128 devices in a mesh: section: 8 (over x, y_lo), seq: 16 (over z, y_hi, core).
Axes of the slice: x: 4, y: 4 (y_hi: 2, y_lo: 2; y = y_hi * 2 + y_lo), z: 4, core: 2. Of those that a mesh axis runs over, the one named last changes fastest.
Arguments:
- inflow: bfloat16 [8, 1024, 4096], P('section', 'seq'), may hold values from -6 to 6
- fresh: bfloat16 [1, 1024, 4096], P(None, 'seq'), may hold values from -6 to 6
- proj_weight: bfloat16 [8, 4096, 640], P('section'), may hold values from -0.09375 to 0.09375
- xz_weight: bfloat16 [8, 4096, 2, 4096], P('section', None, None, 'seq'), may hold values from -0.09375 to 0.09375
- conv_weight: float32 [8, 4, 4608], P('section'), may hold values from -3 to 3
- conv_bias: float32 [8, 4608], P('section'), may hold values from -3 to 3
- step_bias: float32 [8, 128], P('section'), may hold values from -3 to 0
- decay_log: float32 [8, 128], P('section'), may hold values from -7 to -1
- skip_weight: float32 [8, 128], P('section'), may hold values from 0.5 to 1.5
- norm_gain: float32 [8, 4096], P('section'), may hold values from 0.5 to 1.5
- out_weight: bfloat16 [8, 4096, 4096], P('section', 'seq'), may hold values from -0.09375 to 0.09375
Outputs:
- section_outputs: float32 [8, 2, 1024, 4096], P('section', None, 'seq')
The draws below stay inside these ranges and needn't reach their ends.
All inputs are finite; a program needn't handle non-finite values.
Results may differ from the reference program's by a relative error of at most 0.014.
Values may be sent and summed in bfloat16 or wider, within the bound.
A program may use at most 128 MiB of HBM per device.

```python
import jax
import jax.numpy as jnp
from jax import lax

D = 4096
HEADS = 128
HEAD_DIM = 32
STATE = 64
GROUPS = 4
CONV = 4
BLOCK = 128
WINDOW = 2
INNER = 4096
PROJ = 640
CONVCH = 4608
LENGTH = 1024
SECTIONS = 8


def steps_of(stream_key, extent, split, least, high):
    def one(axis_at, parts):
        steps = jax.random.uniform(jax.random.fold_in(jax.random.fold_in(stream_key, 6), axis_at), (parts,), jnp.float32, least / len(split), high / len(split))
        return jnp.repeat(jnp.exp(steps), extent[axis_at] // parts).reshape((-1,) + (1,) * (len(extent) - axis_at - 1))

    factor_of = one(*split[0])
    for cut in split[1:]:
        factor_of = factor_of * one(*cut)
    return factor_of


def scatter_about(stream_key, extent, spread, bound, split=(), dtype=jnp.bfloat16):
    loudness = steps_of(stream_key, extent, split, -0.22, 0.18) if split else 1.0
    entries = jax.random.normal(stream_key, extent, jnp.float32) * spread * loudness
    return jnp.minimum(jnp.maximum(entries, -bound), bound).astype(dtype)


def setup_inputs(seed: int = 0) -> dict:
    arg_keys = jax.random.split(jax.random.key(seed), 12)
    return {
        "inflow": scatter_about(arg_keys[0], (SECTIONS, LENGTH, D), 1.0, 6.0, ((0, 8), (1, 16))),
        "fresh": scatter_about(arg_keys[1], (WINDOW - 1, LENGTH, D), 1.0, 6.0, ((1, 16),)),
        "proj_weight": scatter_about(arg_keys[2], (SECTIONS, D, PROJ), D ** -0.5, 0.09375, ((0, 8),)),
        "xz_weight": scatter_about(arg_keys[3], (SECTIONS, D, 2, INNER), D ** -0.5, 0.09375, ((0, 8), (3, 16))),
        "conv_weight": scatter_about(arg_keys[4], (SECTIONS, CONV, CONVCH), CONV ** -0.5, 3.0, ((0, 8),), jnp.float32),
        "conv_bias": scatter_about(arg_keys[5], (SECTIONS, CONVCH), 0.5, 3.0, ((0, 8),), jnp.float32),
        "step_bias": jnp.clip(-3.0 + 3.0 * jax.random.uniform(arg_keys[6], (SECTIONS, HEADS), jnp.float32) ** steps_of(arg_keys[6], (SECTIONS, HEADS), ((0, 8),), -0.2, 0.2), -3.0, 0.0),
        "decay_log": jnp.clip(-7.0 + 6.0 * jax.random.uniform(arg_keys[7], (SECTIONS, HEADS), jnp.float32) ** steps_of(arg_keys[7], (SECTIONS, HEADS), ((0, 8),), -0.2, 0.2), -7.0, -1.0),
        "skip_weight": jnp.clip(0.5 + 1.0 * jax.random.uniform(arg_keys[8], (SECTIONS, HEADS), jnp.float32) ** steps_of(arg_keys[8], (SECTIONS, HEADS), ((0, 8),), -0.2, 0.2), 0.5, 1.5),
        "norm_gain": jnp.clip(1.0 + 0.1 * jax.random.normal(arg_keys[9], (SECTIONS, INNER), jnp.float32), 0.5, 1.5),
        "out_weight": scatter_about(arg_keys[10], (SECTIONS, INNER, D), INNER ** -0.5, 0.09375, ((0, 8), (1, 16))),
    }


def block_terms(x_block, b_block, c_block, step_block, decay_block):
    cumulus = jnp.cumsum(decay_block, axis=0)
    scores = jnp.einsum('qgn,kgn->gqk', c_block.astype(jnp.float32), b_block.astype(jnp.float32))
    along = jnp.moveaxis(cumulus, 0, 2)
    row_count = cumulus.shape[0]
    row_index = lax.broadcasted_iota(jnp.int32, (row_count, row_count), 0)
    col_index = lax.broadcasted_iota(jnp.int32, (row_count, row_count), 1)
    log_gap = jnp.where(row_index >= col_index, along[..., :, None] - along[..., None, :], -1e+30)
    step_along = jnp.moveaxis(step_block, 0, 2)
    mixing = (scores[:, None] * jnp.exp(log_gap) * step_along[..., None, :]).astype(jnp.bfloat16)
    mixing = lax.optimization_barrier(mixing).astype(jnp.float32)
    diagonal_out = jnp.einsum('gjqk,kgjp->qgjp', mixing, x_block.astype(jnp.float32))
    block_total = cumulus[-1]
    weighted = (x_block.astype(jnp.float32) * (jnp.exp(block_total[None] - cumulus) * step_block)[..., None]).astype(jnp.bfloat16)
    weighted = lax.optimization_barrier(weighted).astype(jnp.float32)
    block_state = jnp.einsum('kgjp,kgn->gjpn', weighted, b_block.astype(jnp.float32))
    return (diagonal_out, cumulus, block_total, block_state)

def run_block(state, pieces):
    x_block, b_block, c_block, step_block, decay_block = pieces
    diagonal_out, cumulus, block_total, block_state = block_terms(x_block, b_block, c_block, step_block, decay_block)
    entering = lax.optimization_barrier(state.astype(jnp.bfloat16)).astype(jnp.float32)
    off_out = jnp.einsum('qgn,gjpn->qgjp', c_block.astype(jnp.float32), entering) * jnp.exp(cumulus)[..., None]
    new_state = jnp.exp(block_total)[..., None, None] * state + block_state
    return (new_state, diagonal_out + off_out)

def mamba_layer(layer_input, proj_w, xz_w, conv_taps, conv_offset, bias_steps, rate_log, skip_gain, out_gain, out_w):
    tokens = layer_input.shape[0]
    inner = HEADS * HEAD_DIM
    bc_width = GROUPS * STATE
    per_group = HEADS // GROUPS
    xz_both = jnp.dot(layer_input, xz_w.reshape(D, 2 * inner), preferred_element_type=jnp.float32).astype(jnp.bfloat16)
    projected = jnp.dot(layer_input, proj_w, preferred_element_type=jnp.float32).astype(jnp.bfloat16)
    joined = jnp.concatenate([xz_both[:, inner:], projected[:, :2 * bc_width]], axis=1)
    padded = jnp.concatenate([jnp.zeros((CONV - 1, joined.shape[1]), jnp.bfloat16), joined], axis=0)
    conv_sum = conv_offset + conv_taps[0] * padded[0:tokens].astype(jnp.float32)
    for offset in range(1, CONV):
        conv_sum = conv_sum + conv_taps[offset] * padded[offset:offset + tokens].astype(jnp.float32)
    convolved = jax.nn.silu(conv_sum).astype(jnp.bfloat16)
    block_count = tokens // BLOCK
    x_blocks = convolved[:, :inner].reshape(block_count, BLOCK, GROUPS, per_group, HEAD_DIM)
    b_blocks = convolved[:, inner:inner + bc_width].reshape(block_count, BLOCK, GROUPS, STATE)
    c_blocks = convolved[:, inner + bc_width:].reshape(block_count, BLOCK, GROUPS, STATE)
    step_size = jax.nn.softplus(projected[:, 2 * bc_width:].astype(jnp.float32) + bias_steps)
    log_decay = -jnp.exp(rate_log) * step_size
    step_blocks = step_size.reshape(block_count, BLOCK, GROUPS, per_group)
    decay_blocks = log_decay.reshape(block_count, BLOCK, GROUPS, per_group)
    start_state = jnp.zeros((GROUPS, per_group, HEAD_DIM, STATE), jnp.float32)
    _, scanned = lax.scan(run_block, start_state, (x_blocks, b_blocks, c_blocks, step_blocks, decay_blocks))
    x_heads = convolved[:, :inner].reshape(tokens, HEADS, HEAD_DIM).astype(jnp.float32)
    mixed = scanned.reshape(tokens, HEADS, HEAD_DIM) + skip_gain[:, None] * x_heads
    gated = mixed.reshape(tokens, inner) * jax.nn.silu(xz_both[:, :inner].astype(jnp.float32))
    grouped = gated.reshape(tokens, GROUPS, inner // GROUPS)
    mean_square = lax.optimization_barrier(jnp.mean(grouped * grouped, axis=2, keepdims=True))
    normed = ((grouped * lax.rsqrt(mean_square + 1e-05)).reshape(tokens, inner) * out_gain).astype(jnp.bfloat16)
    return jnp.dot(normed, out_w, preferred_element_type=jnp.float32)

def run_section(pieces):
    return mamba_layer(*pieces)

def reference(inflow, fresh, proj_weight, xz_weight, conv_weight, conv_bias, step_bias, decay_log, skip_weight, norm_gain, out_weight):
    params = (proj_weight, xz_weight, conv_weight, conv_bias, step_bias, decay_log, skip_weight, norm_gain, out_weight)
    current = inflow
    results = []
    for window_step in range(WINDOW):
        stacked = lax.map(run_section, (current,) + params)
        results.append(stacked)
        if window_step + 1 < WINDOW:
            current = jnp.concatenate([fresh[window_step][None], stacked[:-1].astype(jnp.bfloat16)], axis=0)
    return jnp.stack(results, axis=1)
```

```python
import functools

import jax
import jax.numpy as jnp
from jax import lax
from jax.experimental import pallas as pl
from jax.experimental.pallas import tpu as pltpu
from jax.sharding import PartitionSpec as P

MESH = pl.DeviceIdType.MESH
F32 = jnp.float32
BF16 = jnp.bfloat16
HIGHEST = lax.Precision.HIGHEST
TOKENS = 1024
WIDTH = 4096
CHAN = 256
BLOCK = 128
PIECE = 32
COLS = 896
MIB = 2**20


def place():
    sec = lax.axis_index("section")
    me = lax.axis_index("seq")
    z, h, c = me // 4, (me // 2) % 2, me % 2
    return sec, z, h, c


class Copies:
    def __init__(self, send_sem, recv_sem):
        self.send_sem, self.recv_sem = send_sem, recv_sem
        self.made = []

    def new(self, src, dst, target):
        index = len(self.made)
        copy = pltpu.make_async_remote_copy(
            src_ref=src,
            dst_ref=dst,
            send_sem=self.send_sem.at[index],
            recv_sem=self.recv_sem.at[index],
            device_id=target,
            device_id_type=MESH,
        )
        copy.start()
        self.made.append(copy)
        return copy

    def finish(self):
        for copy in self.made:
            copy.wait_send()


def meet(targets):
    barrier = pltpu.get_barrier_semaphore()
    for target in targets:
        pl.semaphore_signal(barrier, inc=1, device_id=target, device_id_type=MESH)
    pl.semaphore_wait(barrier, len(targets))


def gather_kernel(shard, wxz, wproj, out, act, weight, send_sem, recv_sem, local_sem):
    sec, z, h, c = place()
    zp, zm, zz, hh = (z + 1) % 4, (z + 3) % 4, (z + 2) % 4, 1 - h

    def dev(z_, h_, c_):
        return (sec, z_ * 4 + h_ * 2 + c_)

    up, down, across, sib = dev(zp, h, c), dev(zm, h, c), dev(z, hh, c), dev(z, h, 1 - c)
    pair = z // 2
    loads = []
    for index, (src, dst) in enumerate(
        [
            (shard, act.at[pl.ds(pl.multiple_of((z * 4 + h * 2 + c) * 64, 64), 64)]),
            (wxz, weight.at[:, pl.ds(0, 2 * CHAN)]),
            (wproj.at[:, pl.ds(pl.multiple_of(pair * 128, 128), 128)], weight.at[:, pl.ds(512, 128)]),
            (wproj.at[:, pl.ds(pl.multiple_of(256 + pair * 128, 128), 128)], weight.at[:, pl.ds(640, 128)]),
            (wproj.at[:, pl.ds(512, 128)], weight.at[:, pl.ds(768, 128)]),
        ]
    ):
        load = pltpu.make_async_copy(src, dst, local_sem.at[index])
        load.start()
        loads.append(load)
    meet([up, down, across, sib])
    copies = Copies(send_sem, recv_sem)

    def rows(z_, h_, p):
        start = pl.multiple_of((z_ * 2 + h_) * 128 + c * 64 + p * PIECE, PIECE)
        return act.at[pl.ds(start, PIECE)]

    def own(p):
        return shard.at[pl.ds(p * PIECE, PIECE)]

    def forward(z_, h_, p, target):
        return copies.new(rows(z_, h_, p), rows(z_, h_, p), target)

    def project(z_, h_):
        start = pl.multiple_of((z_ * 2 + h_) * 128, 128)
        for first, size in ((0, 256), (256, 256), (512, 256), (768, 128)):
            out[pl.ds(start, 128), pl.ds(first, size)] = jnp.dot(
                act[pl.ds(start, 128), :], weight[:, pl.ds(first, size)], preferred_element_type=F32
            ).astype(BF16)

    to_up, to_down, to_across, to_sib = [None] * 2, [None] * 2, [None] * 2, [None] * 2
    for p in (0, 1):
        to_up[p] = copies.new(own(p), rows(z, h, p), up)
        to_down[1 - p] = copies.new(own(1 - p), rows(z, h, 1 - p), down)
        to_across[p] = copies.new(own(p), rows(z, h, p), across)
        to_sib[p] = copies.new(own(p), rows(z, h, p), sib)

    for load in loads:
        load.wait()
    for p in (0, 1):
        to_sib[p].wait_recv()
    project(z, h)

    to_up[0].wait_recv()
    c_up = forward(zm, h, 0, up)
    s_zm = [forward(zm, h, 0, sib), None]
    to_down[1].wait_recv()
    c_down = forward(zp, h, 1, down)
    s_zp = [None, forward(zp, h, 1, sib)]
    p_up, p_down, s_p = [None] * 2, [None] * 2, [None] * 2
    to_across[0].wait_recv()
    p_up[0] = forward(z, hh, 0, up)
    p_down[0] = forward(z, hh, 0, down)
    s_p[0] = forward(z, hh, 0, sib)
    to_up[1].wait_recv()
    s_zm[1] = forward(zm, h, 1, sib)
    to_down[0].wait_recv()
    s_zp[0] = forward(zp, h, 0, sib)
    to_across[1].wait_recv()
    p_up[1] = forward(z, hh, 1, up)
    p_down[1] = forward(z, hh, 1, down)
    s_p[1] = forward(z, hh, 1, sib)
    for p in (0, 1):
        s_zm[p].wait_recv()
    project(zm, h)
    c_up.wait_recv()
    c_y, s_c = [None] * 2, [None] * 2
    c_y[0] = forward(zz, h, 0, across)
    s_c[0] = forward(zz, h, 0, sib)
    c_down.wait_recv()
    c_y[1] = forward(zz, h, 1, across)
    s_c[1] = forward(zz, h, 1, sib)
    for p in (0, 1):
        s_zp[p].wait_recv()
    project(zp, h)
    for p in (0, 1):
        s_p[p].wait_recv()
    project(z, hh)
    s_pm, s_pp = [None] * 2, [None] * 2
    for p in (0, 1):
        p_up[p].wait_recv()
        s_pm[p] = forward(zm, hh, p, sib)
        p_down[p].wait_recv()
        s_pp[p] = forward(zp, hh, p, sib)
        if p == 0:
            for q in (0, 1):
                s_c[q].wait_recv()
            project(zz, h)
    for p in (0, 1):
        s_pm[p].wait_recv()
    project(zm, hh)
    s_cy = [None] * 2
    for p in (0, 1):
        c_y[p].wait_recv()
        s_cy[p] = forward(zz, hh, p, sib)
    for p in (0, 1):
        s_pp[p].wait_recv()
    project(zp, hh)
    for p in (0, 1):
        s_cy[p].wait_recv()
    project(zz, hh)
    copies.finish()


def gather_project(shard, wxz, wproj):
    return pl.pallas_call(
        gather_kernel,
        out_shape=jax.ShapeDtypeStruct((TOKENS, COLS), BF16),
        in_specs=[pl.BlockSpec(memory_space=pl.ANY)] * 3,
        out_specs=pl.BlockSpec(memory_space=pltpu.VMEM),
        scratch_shapes=[
            pltpu.VMEM((TOKENS, WIDTH), BF16),
            pltpu.VMEM((WIDTH, COLS), BF16),
            pltpu.SemaphoreType.DMA((30,)),
            pltpu.SemaphoreType.DMA((30,)),
            pltpu.SemaphoreType.DMA((5,)),
        ],
        compiler_params=pltpu.CompilerParams(
            collective_id=0, has_side_effects=True, vmem_limit_bytes=40 * MIB
        ),
        name="gather_project",
    )(shard, wxz, wproj)


def scan_kernel(proj, conv_w, conv_b, step_b, decay, skip, gain, out, squares, window, state):
    me = lax.axis_index("seq")
    group = me // 4
    x_at = pl.multiple_of(me * CHAN, CHAN)
    b_at = pl.multiple_of(4096 + (group // 2) * 128, 128)
    c_at = pl.multiple_of(4352 + (group // 2) * 128, 128)

    def own(ref):
        return jnp.concatenate(
            [ref[:, pl.ds(x_at, CHAN)], ref[:, pl.ds(b_at, 128)], ref[:, pl.ds(c_at, 128)]], axis=1
        )

    def iota(shape, dim):
        return lax.broadcasted_iota(jnp.int32, shape, dim)

    taps = own(conv_w)
    offset = own(conv_b)
    spread = (iota((128, CHAN), 0) == me * 8 + iota((128, CHAN), 1) // 32).astype(F32)

    def per_channel(ref):
        return jnp.dot(
            jnp.broadcast_to(ref[...], (8, 128)), spread, precision=HIGHEST, preferred_element_type=F32
        )[0:1]

    bias = per_channel(step_b)
    rate = -jnp.exp(per_channel(decay))
    direct = per_channel(skip)
    gains = gain[:, pl.ds(x_at, CHAN)]
    lower = iota((BLOCK, BLOCK), 0) >= iota((BLOCK, BLOCK), 1)
    lower_ones = lower.astype(F32)
    own_half = iota((BLOCK, 128), 1) // 64 == group % 2
    head_of = iota((BLOCK, CHAN), 1) // 32
    spread16 = spread.astype(BF16)

    window[0:8, :] = jnp.zeros((8, 512), F32)
    state[...] = jnp.zeros_like(state)

    def block(index, carry):
        at = pl.ds(pl.multiple_of(index * BLOCK, BLOCK), BLOCK)
        window[8 : 8 + BLOCK, :] = proj[at, pl.ds(256, 512)].astype(F32)
        conv = offset + taps[0:1] * window[5 : 5 + BLOCK, :]
        for k in range(1, 4):
            conv = conv + taps[k : k + 1] * window[5 + k : 5 + k + BLOCK, :]
        window[0:8, :] = window[BLOCK : BLOCK + 8, :]
        conv = (conv / (1.0 + jnp.exp(-conv))).astype(BF16)
        x = conv[:, :CHAN]
        b = conv[:, CHAN : CHAN + 128]
        c = jnp.where(own_half, conv[:, CHAN + 128 :], jnp.zeros((), BF16))
        step = jax.nn.softplus(
            jnp.dot(proj[at, pl.ds(768, 128)], spread16, preferred_element_type=F32) + bias
        )
        cumulus = jnp.dot(lower_ones, rate * step, precision=HIGHEST, preferred_element_type=F32)
        total = cumulus[BLOCK - 1 : BLOCK]
        cumulus_t = cumulus.T
        step_t = step.T
        scores = lax.dot_general(c, b, (((1,), (1,)), ((), ())), preferred_element_type=F32)
        mixing, values = [], []
        for head in range(8):
            lane = 32 * head
            gap = cumulus[:, lane : lane + 1] - cumulus_t[lane : lane + 1, :]
            gap = jnp.where(lower, gap, -1e30)
            mixing.append((scores * jnp.exp(gap) * step_t[lane : lane + 1, :]).astype(BF16))
            values.append(jnp.where(head_of == head, x, jnp.zeros((), BF16)))
        mixed = jnp.dot(
            jnp.concatenate(mixing, axis=1), jnp.concatenate(values, axis=0), preferred_element_type=F32
        )
        x32 = x.astype(F32)
        before = state[...]
        mixed = mixed + jnp.exp(cumulus) * jnp.dot(c, before.astype(BF16), preferred_element_type=F32)
        mixed = mixed + direct * x32
        weighted = (x32 * (jnp.exp(total - cumulus) * step)).astype(BF16)
        state[...] = jnp.exp(total) * before + lax.dot_general(
            b, weighted, (((0,), (0,)), ((), ())), preferred_element_type=F32
        )
        gate = proj[at, pl.ds(0, CHAN)].astype(F32)
        gated = mixed * (gate / (1.0 + jnp.exp(-gate)))
        squares[:, at] = lax.dot_general(
            jnp.ones((8, CHAN), F32),
            gated * gated,
            (((1,), (1,)), ((), ())),
            precision=HIGHEST,
            preferred_element_type=F32,
        )
        out[at, :] = (gated * gains).astype(BF16)
        return carry

    lax.fori_loop(0, TOKENS // BLOCK, block, 0)


def scan_gate(proj, conv_w, conv_b, step_b, decay, skip, gain):
    return pl.pallas_call(
        scan_kernel,
        out_shape=(
            jax.ShapeDtypeStruct((TOKENS, CHAN), BF16),
            jax.ShapeDtypeStruct((8, TOKENS), F32),
        ),
        in_specs=[pl.BlockSpec(memory_space=pltpu.VMEM)] * 7,
        out_specs=(pl.BlockSpec(memory_space=pltpu.VMEM),) * 2,
        scratch_shapes=[pltpu.VMEM((BLOCK + 8, 512), F32), pltpu.VMEM((128, CHAN), F32)],
        compiler_params=pltpu.CompilerParams(vmem_limit_bytes=40 * MIB),
        name="scan_gate",
    )(proj, conv_w, conv_b, step_b, decay, skip, gain)


def scatter_kernel(relay, gated, squares, wout, *refs):
    if relay:
        out, passed = refs[:2]
        refs = refs[2:]
    else:
        out = refs[0]
        refs = refs[1:]
    part, from_sib, got, stats, scale, staged, send_sem, recv_sem = refs
    sec, z, h, c = place()
    zp, zm, zz, hh = (z + 1) % 4, (z + 3) % 4, (z + 2) % 4, 1 - h

    def dev(z_, h_, c_):
        return (sec, z_ * 4 + h_ * 2 + c_)

    up, down, across, sib = dev(zp, h, c), dev(zm, h, c), dev(z, hh, c), dev(z, h, 1 - c)
    diag = dev(z, hh, 1 - c)
    here = z * 4 + h * 2 + c
    after, ahead = ((sec + 1) % 8, here), ((sec + 7) % 8, here)
    meet([up, down, across, sib, diag] + ([after, ahead] if relay else []))
    copies = Copies(send_sem, recv_sem)

    shares = [copies.new(squares, stats.at[i], t) for i, t in enumerate((sib, across, diag))]
    for share in shares:
        share.wait_recv()
    mean = (squares[...] + stats[0] + stats[1] + stats[2]) / 1024.0
    factor = lax.rsqrt(mean + 1e-05)
    for i in range(TOKENS // BLOCK):
        scale[pl.ds(i * BLOCK, BLOCK), :] = lax.dot_general(
            factor[:, i * BLOCK : (i + 1) * BLOCK],
            jnp.full((8, 128), 0.125, F32),
            (((0,), (0,)), ((), ())),
            precision=HIGHEST,
            preferred_element_type=F32,
        )

    def mine(z_, h_, p):
        start = pl.multiple_of((z_ * 2 + h_) * 128 + c * 64 + p * PIECE, PIECE)
        return part.at[pl.ds(start, PIECE)]

    def compute(z_, h_):
        start = pl.multiple_of((z_ * 2 + h_) * 128, 128)
        at = pl.ds(start, 128)
        rows_scale = jnp.concatenate([scale[at, :]] * 4, axis=1)
        lhs = gated[at, :]

        def tile(n, carry):
            cols = pl.ds(pl.multiple_of(n * 512, 512), 512)
            part[at, cols] = (
                jnp.dot(lhs, wout[:, cols], preferred_element_type=F32) * rows_scale
            ).astype(BF16)
            return carry

        lax.fori_loop(0, WIDTH // 512, tile, 0)
        src = part.at[pl.ds(pl.multiple_of(start + (1 - c) * 64, 64), 64)]
        dst = from_sib.at[pl.ds(pl.multiple_of((z_ * 2 + h_) * 64, 64), 64)]
        return copies.new(src, dst, sib)

    def add(dst, *others):
        def tile(n, carry):
            cols = pl.ds(pl.multiple_of(n * 512, 512), 512)
            total = dst[:, cols].astype(F32)
            for other in others:
                total = total + other[:, cols].astype(F32)
            dst[:, cols] = total.astype(BF16)
            return carry

        lax.fori_loop(0, WIDTH // 512, tile, 0)

    def paired(z_, h_, copy):
        copy.wait_recv()
        for p in (0, 1):
            start = pl.multiple_of((z_ * 2 + h_) * 64 + p * PIECE, PIECE)
            add(mine(z_, h_, p), from_sib.at[pl.ds(start, PIECE)])

    s0 = compute(zz, hh)
    s1 = compute(zp, hh)
    paired(zz, hh, s0)
    y1 = [copies.new(mine(zz, hh, p), got.at[p], across) for p in (0, 1)]
    s2 = compute(zm, hh)
    paired(zp, hh, s1)
    u5 = [copies.new(mine(zp, hh, p), got.at[2 + p], up) for p in (0, 1)]
    s3 = compute(zz, h)
    paired(zm, hh, s2)
    d5 = [copies.new(mine(zm, hh, p), got.at[4 + p], down) for p in (0, 1)]
    s4 = compute(zp, h)
    paired(zz, h, s3)
    s5 = compute(zm, h)
    paired(zp, h, s4)
    u4 = [copies.new(mine(zp, h, 0), got.at[6], up), None]
    s6 = compute(z, hh)
    paired(zm, h, s5)
    d4 = [None, copies.new(mine(zm, h, 1), got.at[9], down)]
    s7 = compute(z, h)
    paired(z, hh, s6)
    paired(z, h, s7)

    y1[0].wait_recv()
    add(mine(zz, h, 0), got.at[0])
    c_down = copies.new(mine(zz, h, 0), got.at[10], down)
    y1[1].wait_recv()
    add(mine(zz, h, 1), got.at[1])
    c_up = copies.new(mine(zz, h, 1), got.at[11], up)
    y6 = [None] * 2
    for p in (0, 1):
        u5[p].wait_recv()
        d5[p].wait_recv()
        add(mine(z, hh, p), got.at[2 + p], got.at[4 + p])
        y6[p] = copies.new(mine(z, hh, p), got.at[12 + p], across)
    c_down.wait_recv()
    add(mine(zm, h, 0), got.at[10])
    d4[0] = copies.new(mine(zm, h, 0), got.at[8], down)
    c_up.wait_recv()
    add(mine(zp, h, 1), got.at[11])
    u4[1] = copies.new(mine(zp, h, 1), got.at[7], up)

    relays = []
    for p in (0, 1):
        u4[p].wait_recv()
        d4[p].wait_recv()
        y6[p].wait_recv()
        own = mine(z, h, p)
        at = pl.ds(p * PIECE, PIECE)

        def tile(n, carry):
            cols = pl.ds(pl.multiple_of(n * 512, 512), 512)
            total = own[:, cols].astype(F32) + got[12 + p, :, cols].astype(F32)
            total = total + got[6 + p, :, cols].astype(F32) + got[8 + p, :, cols].astype(F32)
            out[at, cols] = total
            if relay:
                staged[at, cols] = total.astype(BF16)
            return carry

        lax.fori_loop(0, WIDTH // 512, tile, 0)
        if relay:
            relays.append(copies.new(staged.at[at], passed.at[at], after))
    for hop in relays:
        hop.wait_recv()
    copies.finish()


def project_scatter(relay, gated, squares, wout):
    shapes = [jax.ShapeDtypeStruct((64, WIDTH), F32)]
    if relay:
        shapes.append(jax.ShapeDtypeStruct((64, WIDTH), BF16))
    count = 3 + 8 + 14 + (2 if relay else 0)
    return pl.pallas_call(
        functools.partial(scatter_kernel, relay),
        out_shape=tuple(shapes),
        in_specs=[pl.BlockSpec(memory_space=pltpu.VMEM)] * 3,
        out_specs=(pl.BlockSpec(memory_space=pltpu.VMEM),) * len(shapes),
        scratch_shapes=[
            pltpu.VMEM((TOKENS, WIDTH), BF16),
            pltpu.VMEM((TOKENS // 2, WIDTH), BF16),
            pltpu.VMEM((14, PIECE, WIDTH), BF16),
            pltpu.VMEM((3, 8, TOKENS), F32),
            pltpu.VMEM((TOKENS, 128), F32),
            pltpu.VMEM((64, WIDTH), BF16),
            pltpu.SemaphoreType.DMA((count,)),
            pltpu.SemaphoreType.DMA((count,)),
        ],
        compiler_params=pltpu.CompilerParams(
            collective_id=1 if relay else 2, has_side_effects=True, vmem_limit_bytes=48 * MIB
        ),
        name="project_scatter",
    )(gated, squares, wout)


def on_device(
    inflow,
    fresh,
    proj_weight,
    xz_weight,
    conv_weight,
    conv_bias,
    step_bias,
    decay_log,
    skip_weight,
    norm_gain,
    out_weight,
):
    wxz = xz_weight[0].reshape(WIDTH, 2 * CHAN)
    wproj = proj_weight[0]

    def mixer(shard):
        proj = gather_project(shard, wxz, wproj)
        return scan_gate(
            proj, conv_weight[0], conv_bias, step_bias, decay_log, skip_weight, norm_gain
        )

    first, passed = project_scatter(True, *mixer(inflow[0]), out_weight[0])
    entering = jnp.where(lax.axis_index("section") == 0, fresh[0], passed)
    (second,) = project_scatter(False, *mixer(entering), out_weight[0])
    return jnp.stack([first, second])[None]


def solution(mesh):
    placed = (
        P("section", "seq", None),
        P(None, "seq", None),
        P("section", None, None),
        P("section", None, None, "seq"),
        P("section", None, None),
        P("section", None),
        P("section", None),
        P("section", None),
        P("section", None),
        P("section", None),
        P("section", "seq", None),
    )
    return jax.shard_map(
        on_device,
        mesh=mesh,
        in_specs=placed,
        out_specs=P("section", None, "seq", None),
        check_vma=False,
    )
```

```python
import functools

import jax
import jax.numpy as jnp
from jax import lax
from jax.experimental import pallas as pl
from jax.experimental.pallas import tpu as pltpu
from jax.sharding import PartitionSpec as P

MESH = pl.DeviceIdType.MESH
F32 = jnp.float32
BF16 = jnp.bfloat16
HIGHEST = lax.Precision.HIGHEST
TOKENS = 1024
WIDTH = 4096
CHAN = 256
BLOCK = 128
BLOCKS = TOKENS // BLOCK
ROWS = 64
HALF = WIDTH // 2
COLS = 896
TILES = ((0, 256), (256, 256), (512, 256), (768, 128))
LAST = 7
COPIES = 192
MIB = 2**20


def aligned(value, by):
    return pl.multiple_of(value, by)


def iota(shape, dim):
    return lax.broadcasted_iota(jnp.int32, shape, dim)


def columns(p):
    return pl.ds(p * HALF, HALF)


class Place:
    def __init__(self):
        self.sec = lax.axis_index("section")
        self.me = lax.axis_index("seq")
        self.z, self.h, self.c = self.me // 4, (self.me // 2) % 2, self.me % 2
        self.zp, self.zm, self.zz = (self.z + 1) % 4, (self.z + 3) % 4, (self.z + 2) % 4
        self.hh = 1 - self.h
        self.up = self.device(self.zp, self.h, self.c)
        self.down = self.device(self.zm, self.h, self.c)
        self.across = self.device(self.z, self.hh, self.c)
        self.sib = self.device(self.z, self.h, 1 - self.c)
        self.diag = self.device(self.z, self.hh, 1 - self.c)
        self.after = ((self.sec + 1) % 8, self.me)
        self.ahead = ((self.sec + 7) % 8, self.me)

    def device(self, z, h, c):
        return (self.sec, z * 4 + h * 2 + c)

    def meet(self):
        targets = [self.up, self.down, self.across, self.sib, self.diag, self.after, self.ahead]
        barrier = pltpu.get_barrier_semaphore()
        for target in targets:
            pl.semaphore_signal(barrier, inc=1, device_id=target, device_id_type=MESH)
        pl.semaphore_wait(barrier, len(targets))


class Copies:
    def __init__(self, send_sem, recv_sem):
        self.send_sem, self.recv_sem = send_sem, recv_sem
        self.count = 0
        self.open = []

    def make(self, src, dst, target):
        index = self.count
        self.count += 1
        return pltpu.make_async_remote_copy(
            src_ref=src,
            dst_ref=dst,
            send_sem=self.send_sem.at[index],
            recv_sem=self.recv_sem.at[index],
            device_id=target,
            device_id_type=MESH,
        )

    def new(self, src, dst, target):
        copy = self.make(src, dst, target)
        copy.start()
        self.open.append(copy)
        return copy

    def finish(self):
        for copy in self.open:
            copy.wait_send()
        self.open = []


class Gather:
    def __init__(self, at, copies, source, act, weight, acc, proj):
        self.at, self.copies, self.source = at, copies, source
        self.act, self.weight, self.acc, self.proj = act, weight, acc, proj
        self.got = {}

    def rows(self, z, h, p, half=None):
        start = (z * 2 + h) * 128 + self.at.c * ROWS
        if half is None:
            return self.act.at[pl.ds(aligned(start, ROWS), ROWS), columns(p)]
        return self.act.at[pl.ds(aligned(start + half * 32, 32), 32), columns(p)]

    def forward(self, z, h, p, target, half=None):
        return self.copies.new(self.rows(z, h, p, half), self.rows(z, h, p, half), target)

    def share(self, name, z, h, p, half=None):
        self.got.setdefault((name, p), []).append(self.forward(z, h, p, self.at.sib, half))

    def own(self, p):
        at = self.at
        src = self.source.at[:, columns(p)]
        dst = self.rows(at.z, at.h, p)
        for name, target in (("up", at.up), ("down", at.down), ("across", at.across), ("own", at.sib)):
            self.got[name, p] = [self.copies.new(src, dst, target)]

    def arrived(self, name, p):
        for copy in self.got[name, p]:
            copy.wait_recv()

    def near(self, p):
        at = self.at
        self.arrived("up", p)
        self.got["cu", p] = [self.forward(at.zm, at.h, p, at.up, 0)]
        self.arrived("down", p)
        self.got["cd", p] = [self.forward(at.zp, at.h, p, at.down, 1)]
        self.share("s_zm", at.zm, at.h, p)
        self.share("s_zp", at.zp, at.h, p)
        self.arrived("across", p)
        self.got["pu", p] = [self.forward(at.z, at.hh, p, at.up)]
        self.got["pd", p] = [self.forward(at.z, at.hh, p, at.down)]
        self.share("s_p", at.z, at.hh, p)

    def far(self, p):
        at = self.at
        for name, half in (("cu", 0), ("cd", 1)):
            self.arrived(name, p)
            self.got["cy%d" % half, p] = [self.forward(at.zz, at.h, p, at.across, half)]
            self.share("s_c", at.zz, at.h, p, half)

    def beside(self, p):
        at = self.at
        self.arrived("pu", p)
        self.share("s_pm", at.zm, at.hh, p)
        self.arrived("pd", p)
        self.share("s_pp", at.zp, at.hh, p)

    def last(self, p):
        at = self.at
        for half in (0, 1):
            self.arrived("cy%d" % half, p)
            self.share("s_cy", at.zz, at.hh, p, half)

    def project(self, name, z, h, p):
        self.arrived(name, p)
        at = pl.ds(aligned((z * 2 + h) * 128, 128), 128)
        for first, size in TILES:
            cols = pl.ds(first, size)
            part = jnp.dot(
                self.act[at, columns(p)], self.weight[columns(p), cols], preferred_element_type=F32
            )
            if p == 0:
                self.acc[at, cols] = part
            else:
                self.proj[at, cols] = (self.acc[at, cols] + part).astype(BF16)

    def project_near(self, p):
        at = self.at
        self.project("own", at.z, at.h, p)
        self.project("s_zm", at.zm, at.h, p)
        self.project("s_zp", at.zp, at.h, p)
        self.project("s_p", at.z, at.hh, p)

    def project_beside(self, p):
        at = self.at
        self.project("s_pm", at.zm, at.hh, p)
        self.project("s_pp", at.zp, at.hh, p)

    def rest(self):
        at = self.at
        self.project_near(0)
        self.near(1)
        self.far(0)
        self.project_near(1)
        self.beside(0)
        self.project("s_c", at.zz, at.h, 0)
        self.far(1)
        self.project_beside(0)
        self.last(0)
        self.project("s_c", at.zz, at.h, 1)
        self.beside(1)
        self.project("s_cy", at.zz, at.hh, 0)
        self.project_beside(1)
        self.last(1)
        self.project("s_cy", at.zz, at.hh, 1)


class Mixer:
    def __init__(self, at, params, proj, conved, steps, sums, entering, window, gated, squares):
        self.proj, self.conved, self.steps, self.sums = proj, conved, steps, sums
        self.entering, self.window, self.gated, self.squares = entering, window, gated, squares
        conv_w, conv_b, step_b, decay, skip, gain = params
        group = at.me // 4
        x_at = aligned(at.me * CHAN, CHAN)
        b_at = aligned(4096 + (group // 2) * 128, 128)
        c_at = aligned(4352 + (group // 2) * 128, 128)

        def own(ref):
            return jnp.concatenate(
                [ref[:, pl.ds(x_at, CHAN)], ref[:, pl.ds(b_at, 128)], ref[:, pl.ds(c_at, 128)]], axis=1
            )

        spread = (iota((128, CHAN), 0) == at.me * 8 + iota((128, CHAN), 1) // 32).astype(F32)

        def per_channel(ref):
            wide = jnp.broadcast_to(ref[...], (8, 128))
            return jnp.dot(wide, spread, precision=HIGHEST, preferred_element_type=F32)[0:1]

        self.taps, self.offset = own(conv_w), own(conv_b)
        self.bias = per_channel(step_b)
        self.rate = -jnp.exp(per_channel(decay))
        self.direct = per_channel(skip)
        self.gains = gain[:, pl.ds(x_at, CHAN)]
        self.spread = spread.astype(BF16)
        self.half = group % 2

    def states(self):
        taps, window = self.taps, self.window
        lower_ones = (iota((BLOCK, BLOCK), 0) >= iota((BLOCK, BLOCK), 1)).astype(F32)
        own_half = iota((BLOCK, 128), 1) // 64 == self.half
        window[0:8, :] = jnp.zeros((8, 512), F32)

        def block(index, before):
            at = pl.ds(aligned(index * BLOCK, BLOCK), BLOCK)
            window[8 : 8 + BLOCK, :] = self.proj[at, pl.ds(256, 512)].astype(F32)
            conv = self.offset + taps[0:1] * window[5 : 5 + BLOCK, :]
            for k in range(1, 4):
                conv = conv + taps[k : k + 1] * window[5 + k : 5 + k + BLOCK, :]
            window[0:8, :] = window[BLOCK : BLOCK + 8, :]
            conv = (conv / (1.0 + jnp.exp(-conv))).astype(BF16)
            x = conv[:, :CHAN]
            b = conv[:, CHAN : CHAN + 128]
            c = jnp.where(own_half, conv[:, CHAN + 128 :], jnp.zeros((), BF16))
            self.conved[at, pl.ds(0, CHAN)] = x
            self.conved[at, pl.ds(CHAN, 128)] = b
            self.conved[at, pl.ds(CHAN + 128, 128)] = c
            step = jax.nn.softplus(
                jnp.dot(self.proj[at, pl.ds(768, 128)], self.spread, preferred_element_type=F32)
                + self.bias
            )
            cumulus = jnp.dot(
                lower_ones, self.rate * step, precision=HIGHEST, preferred_element_type=F32
            )
            total = cumulus[BLOCK - 1 : BLOCK]
            self.steps[at, :] = step
            self.sums[at, :] = cumulus
            self.entering[at, :] = before.astype(BF16)
            weighted = (x.astype(F32) * (jnp.exp(total - cumulus) * step)).astype(BF16)
            return jnp.exp(total) * before + lax.dot_general(
                b, weighted, (((0,), (0,)), ((), ())), preferred_element_type=F32
            )

        lax.fori_loop(0, BLOCKS, block, jnp.zeros((128, CHAN), F32))

    def outputs(self, z):
        lower = iota((BLOCK, BLOCK), 0) >= iota((BLOCK, BLOCK), 1)
        head_of = iota((BLOCK, CHAN), 1) // 32

        def block(index, carry):
            at = pl.ds(aligned(z * 256 + index * BLOCK, BLOCK), BLOCK)
            x = self.conved[at, pl.ds(0, CHAN)]
            b = self.conved[at, pl.ds(CHAN, 128)]
            c = self.conved[at, pl.ds(CHAN + 128, 128)]
            cumulus = self.sums[at, :]
            cumulus_t = cumulus.T
            step_t = self.steps[at, :].T
            scores = lax.dot_general(c, b, (((1,), (1,)), ((), ())), preferred_element_type=F32)
            mixing, values = [], []
            for head in range(8):
                lane = 32 * head
                gap = cumulus[:, lane : lane + 1] - cumulus_t[lane : lane + 1, :]
                gap = jnp.where(lower, gap, -1e30)
                mixing.append((scores * jnp.exp(gap) * step_t[lane : lane + 1, :]).astype(BF16))
                values.append(jnp.where(head_of == head, x, jnp.zeros((), BF16)))
            mixed = jnp.dot(
                jnp.concatenate(mixing, axis=1),
                jnp.concatenate(values, axis=0),
                preferred_element_type=F32,
            )
            mixed = mixed + jnp.exp(cumulus) * jnp.dot(
                c, self.entering[at, :], preferred_element_type=F32
            )
            mixed = mixed + self.direct * x.astype(F32)
            gate = self.proj[at, pl.ds(0, CHAN)].astype(F32)
            gated = mixed * (gate / (1.0 + jnp.exp(-gate)))
            self.squares[:, at] = lax.dot_general(
                jnp.ones((8, CHAN), F32),
                gated * gated,
                (((1,), (1,)), ((), ())),
                precision=HIGHEST,
                preferred_element_type=F32,
            )
            self.gated[at, :] = (gated * self.gains).astype(BF16)
            return carry

        lax.fori_loop(0, 2, block, 0)


class Scatter:
    def __init__(self, at, copies, mixer, wout, part, from_sib, got, stats, scale):
        self.at, self.copies, self.mixer, self.wout = at, copies, mixer, wout
        self.part, self.from_sib, self.got, self.stats, self.scale = part, from_sib, got, stats, scale
        self.sent = {}

    def gate(self, z):
        self.mixer.outputs(z)
        cols = pl.ds(aligned(z * 256, 256), 256)
        squares = self.mixer.squares.at[:, cols]
        self.shares = [
            self.copies.new(squares, self.stats.at[i, :, cols], target)
            for i, target in enumerate((self.at.sib, self.at.across, self.at.diag))
        ]
        return z, self.shares

    def factor(self, gate):
        z, shares = gate
        for share in shares:
            share.wait_recv()
        for i in (0, 1):
            at = pl.ds(aligned(z * 256 + i * 128, 128), 128)
            total = self.mixer.squares[:, at] + self.stats[0, :, at]
            total = total + self.stats[1, :, at] + self.stats[2, :, at]
            self.scale[at, :] = lax.dot_general(
                lax.rsqrt(total / 1024.0 + 1e-05),
                jnp.full((8, 128), 0.125, F32),
                (((0,), (0,)), ((), ())),
                precision=HIGHEST,
                preferred_element_type=F32,
            )

    def mine(self, z, h, p, half=None):
        start = (z * 2 + h) * 128 + self.at.c * ROWS
        if half is None:
            return self.part.at[pl.ds(aligned(start, ROWS), ROWS), columns(p)]
        return self.part.at[pl.ds(aligned(start + half * 32, 32), 32), columns(p)]

    def compute(self, z, h, p):
        start = aligned((z * 2 + h) * 128, 128)
        at = pl.ds(start, 128)
        lhs = self.mixer.gated[at, :]

        def tile(n, carry):
            cols = pl.ds(aligned(p * HALF + n * 512, 512), 512)
            self.part[at, cols] = jnp.dot(
                lhs, self.wout[:, cols], preferred_element_type=F32
            ).astype(BF16)
            return carry

        lax.fori_loop(0, HALF // 512, tile, 0)
        src = self.part.at[pl.ds(aligned(start + (1 - self.at.c) * ROWS, ROWS), ROWS), columns(p)]
        dst = self.from_sib.at[pl.ds(aligned((z * 2 + h) * ROWS, ROWS), ROWS), columns(p)]
        return self.copies.new(src, dst, self.at.sib)

    def pair(self, z, h, p, copy):
        copy.wait_recv()
        own = self.mine(z, h, p)
        other = self.from_sib.at[pl.ds(aligned((z * 2 + h) * ROWS, ROWS), ROWS), columns(p)]
        rows = pl.ds(aligned((z * 2 + h) * 128 + self.at.c * ROWS, ROWS), ROWS)
        scale = jnp.concatenate([self.scale[rows, :]] * 2, axis=1)

        def tile(n, carry):
            cols = pl.ds(aligned(n * 256, 256), 256)
            total = own[:, cols].astype(F32) + other[:, cols].astype(F32)
            own[:, cols] = (total * scale).astype(BF16)
            return carry

        lax.fori_loop(0, HALF // 256, tile, 0)

    @staticmethod
    def add(dst, *others):
        def tile(n, carry):
            cols = pl.ds(aligned(n * 256, 256), 256)
            total = dst[:, cols].astype(F32)
            for other in others:
                total = total + other[:, cols].astype(F32)
            dst[:, cols] = total.astype(BF16)
            return carry

        lax.fori_loop(0, HALF // 256, tile, 0)

    def send(self, name, src, slot, p, target, half=None):
        dst = self.got.at[p, slot]
        if half is not None:
            dst = self.got.at[p, slot, pl.ds(half * 32, 32)]
        self.sent.setdefault((name, p), []).append(self.copies.new(src, dst, target))

    def arrived(self, name, p):
        for copy in self.sent[name, p]:
            copy.wait_recv()

    def first(self):
        at = self.at
        g_zz = self.gate(at.zz)
        c_zzhh = self.compute(at.zz, at.hh, 0)
        g_zp = self.gate(at.zp)
        self.factor(g_zz)
        self.pair(at.zz, at.hh, 0, c_zzhh)
        self.send("y1", self.mine(at.zz, at.hh, 0), 0, 0, at.across)
        c_zphh = self.compute(at.zp, at.hh, 0)
        g_zm = self.gate(at.zm)
        self.factor(g_zp)
        self.pair(at.zp, at.hh, 0, c_zphh)
        self.send("u5", self.mine(at.zp, at.hh, 0), 1, 0, at.up)
        c_zmhh = self.compute(at.zm, at.hh, 0)
        c_zzh = self.compute(at.zz, at.h, 0)
        c_zph = self.compute(at.zp, at.h, 0)
        self.factor(g_zm)
        self.pair(at.zm, at.hh, 0, c_zmhh)
        self.send("d5", self.mine(at.zm, at.hh, 0), 2, 0, at.down)
        self.pair(at.zz, at.h, 0, c_zzh)
        self.pair(at.zp, at.h, 0, c_zph)
        self.send("u4", self.mine(at.zp, at.h, 0, 0), 3, 0, at.up, 0)
        c_zmh = self.compute(at.zm, at.h, 0)
        g_z = self.gate(at.z)
        self.pair(at.zm, at.h, 0, c_zmh)
        self.send("d4", self.mine(at.zm, at.h, 0, 1), 4, 0, at.down, 1)
        c_zhh = self.compute(at.z, at.hh, 0)
        c_zh = self.compute(at.z, at.h, 0)
        self.factor(g_z)
        self.pair(at.z, at.hh, 0, c_zhh)
        self.pair(at.z, at.h, 0, c_zh)

    def second(self):
        at = self.at
        c_zzhh = self.compute(at.zz, at.hh, 1)
        c_zphh = self.compute(at.zp, at.hh, 1)
        c_zmhh = self.compute(at.zm, at.hh, 1)
        self.cross(0)
        self.pair(at.zz, at.hh, 1, c_zzhh)
        self.send("y1", self.mine(at.zz, at.hh, 1), 0, 1, at.across)
        self.pair(at.zp, at.hh, 1, c_zphh)
        self.send("u5", self.mine(at.zp, at.hh, 1), 1, 1, at.up)
        self.pair(at.zm, at.hh, 1, c_zmhh)
        self.send("d5", self.mine(at.zm, at.hh, 1), 2, 1, at.down)
        self.side(0)
        c_zzh = self.compute(at.zz, at.h, 1)
        c_zph = self.compute(at.zp, at.h, 1)
        c_zmh = self.compute(at.zm, at.h, 1)
        self.pair(at.zz, at.h, 1, c_zzh)
        self.join(0)
        self.pair(at.zp, at.h, 1, c_zph)
        self.send("u4", self.mine(at.zp, at.h, 1, 0), 3, 1, at.up, 0)
        self.pair(at.zm, at.h, 1, c_zmh)
        self.send("d4", self.mine(at.zm, at.h, 1, 1), 4, 1, at.down, 1)
        c_zhh = self.compute(at.z, at.hh, 1)
        c_zh = self.compute(at.z, at.h, 1)
        self.pair(at.z, at.hh, 1, c_zhh)
        self.pair(at.z, at.h, 1, c_zh)

    def cross(self, p):
        at = self.at
        self.arrived("y1", p)
        self.add(self.mine(at.zz, at.h, p), self.got.at[p, 0])
        self.send("c_down", self.mine(at.zz, at.h, p, 0), 5, p, at.down, 0)
        self.send("c_up", self.mine(at.zz, at.h, p, 1), 5, p, at.up, 1)

    def side(self, p):
        at = self.at
        self.arrived("u5", p)
        self.arrived("d5", p)
        self.add(self.mine(at.z, at.hh, p), self.got.at[p, 1], self.got.at[p, 2])
        self.send("y6", self.mine(at.z, at.hh, p), 6, p, at.across)

    def join(self, p):
        at = self.at
        self.arrived("c_down", p)
        self.add(self.mine(at.zm, at.h, p, 0), self.got.at[p, 5, pl.ds(0, 32)])
        self.send("d4", self.mine(at.zm, at.h, p, 0), 4, p, at.down, 0)
        self.arrived("c_up", p)
        self.add(self.mine(at.zp, at.h, p, 1), self.got.at[p, 5, pl.ds(32, 32)])
        self.send("u4", self.mine(at.zp, at.h, p, 1), 3, p, at.up, 1)

    def total(self, p, out, staged):
        at = self.at
        for name in ("y6", "u4", "d4"):
            self.arrived(name, p)
        own = self.mine(at.z, at.h, p)

        def tile(n, carry):
            cols = pl.ds(aligned(n * 256, 256), 256)
            wide = pl.ds(aligned(p * HALF + n * 256, 256), 256)
            total = own[:, cols].astype(F32) + self.got[p, 6, :, cols].astype(F32)
            total = total + self.got[p, 3, :, cols].astype(F32) + self.got[p, 4, :, cols].astype(F32)
            out[:, wide] = total
            if staged is not None:
                staged[:, wide] = total.astype(BF16)
            return carry

        lax.fori_loop(0, HALF // 256, tile, 0)


def kernel(
    inflow, fresh, wxz, wproj, wout, conv_w, conv_b, step_b, decay, skip, gain, out,
    act, weight, acc, proj, conved, steps, sums, entering, window, gated, squares,
    part, from_sib, got, stats, scale, staged, received, send_sem, recv_sem, local_sem,
):
    at = Place()
    pair = at.z // 2
    here = pl.ds(aligned(at.me * ROWS, ROWS), ROWS)
    loads = []
    for index, (src, dst) in enumerate(
        [
            (inflow, act.at[here]),
            (wxz, weight.at[:, pl.ds(0, 2 * CHAN)]),
            (wproj.at[:, pl.ds(aligned(pair * 128, 128), 128)], weight.at[:, pl.ds(512, 128)]),
            (wproj.at[:, pl.ds(aligned(256 + pair * 128, 128), 128)], weight.at[:, pl.ds(640, 128)]),
            (wproj.at[:, pl.ds(512, 128)], weight.at[:, pl.ds(768, 128)]),
        ]
    ):
        load = pltpu.make_async_copy(src, dst, local_sem.at[index])
        load.start()
        loads.append(load)
    at.meet()
    copies = Copies(send_sem, recv_sem)
    mixer = Mixer(
        at, (conv_w, conv_b, step_b, decay, skip, gain),
        proj, conved, steps, sums, entering, window, gated, squares,
    )
    scatter_refs = (wout, part, from_sib, got, stats, scale)

    gather = Gather(at, copies, inflow, act, weight, acc, proj)
    gather.own(0)
    gather.own(1)
    for load in loads:
        load.wait()

    @pl.when(at.sec == 0)
    def _():
        load = pltpu.make_async_copy(fresh, received, local_sem.at[0])
        load.start()
        load.wait()

    gather.near(0)
    gather.rest()
    mixer.states()
    copies.finish()

    scatter = Scatter(at, copies, mixer, *scatter_refs)
    hops = [copies.make(staged.at[:, columns(p)], received.at[:, columns(p)], at.after) for p in (0, 1)]

    def relay(p):
        scatter.total(p, out.at[0], staged)
        pl.when(at.sec < LAST)(hops[p].start)

    def relayed(p):
        pl.when(at.sec > 0)(hops[p].wait_recv)
        keep = pltpu.make_async_copy(
            received.at[:, columns(p)], act.at[here, columns(p)], local_sem.at[p]
        )
        keep.start()
        gather.own(p)
        return keep

    scatter.first()
    scatter.second()
    relay(0)
    scatter.cross(1)
    scatter.side(1)
    gather = Gather(at, copies, received, act, weight, acc, proj)
    keeps = [relayed(0)]
    scatter.join(1)
    relay(1)
    gather.near(0)
    keeps.append(relayed(1))
    for keep in keeps:
        keep.wait()
    gather.rest()
    mixer.states()
    for p in (0, 1):
        pl.when(at.sec < LAST)(hops[p].wait_send)
    copies.finish()

    scatter = Scatter(at, copies, mixer, *scatter_refs)
    scatter.first()
    scatter.second()
    scatter.total(0, out.at[1], None)
    scatter.cross(1)
    scatter.side(1)
    scatter.join(1)
    scatter.total(1, out.at[1], None)
    copies.finish()


def on_device(
    inflow,
    fresh,
    proj_weight,
    xz_weight,
    conv_weight,
    conv_bias,
    step_bias,
    decay_log,
    skip_weight,
    norm_gain,
    out_weight,
):
    anywhere = pl.BlockSpec(memory_space=pl.ANY)
    vmem = pl.BlockSpec(memory_space=pltpu.VMEM)
    out = pl.pallas_call(
        kernel,
        out_shape=jax.ShapeDtypeStruct((2, ROWS, WIDTH), F32),
        in_specs=[anywhere] * 4 + [vmem] * 7,
        out_specs=vmem,
        scratch_shapes=[
            pltpu.VMEM((TOKENS, WIDTH), BF16),
            pltpu.VMEM((WIDTH, COLS), BF16),
            pltpu.VMEM((TOKENS, COLS), F32),
            pltpu.VMEM((TOKENS, COLS), BF16),
            pltpu.VMEM((TOKENS, 512), BF16),
            pltpu.VMEM((TOKENS, CHAN), F32),
            pltpu.VMEM((TOKENS, CHAN), F32),
            pltpu.VMEM((TOKENS, CHAN), BF16),
            pltpu.VMEM((BLOCK + 8, 512), F32),
            pltpu.VMEM((TOKENS, CHAN), BF16),
            pltpu.VMEM((8, TOKENS), F32),
            pltpu.VMEM((TOKENS, WIDTH), BF16),
            pltpu.VMEM((TOKENS // 2, WIDTH), BF16),
            pltpu.VMEM((2, LAST, ROWS, HALF), BF16),
            pltpu.VMEM((3, 8, TOKENS), F32),
            pltpu.VMEM((TOKENS, 128), F32),
            pltpu.VMEM((ROWS, WIDTH), BF16),
            pltpu.VMEM((ROWS, WIDTH), BF16),
            pltpu.SemaphoreType.DMA((COPIES,)),
            pltpu.SemaphoreType.DMA((COPIES,)),
            pltpu.SemaphoreType.DMA((5,)),
        ],
        compiler_params=pltpu.CompilerParams(
            collective_id=0, has_side_effects=True, vmem_limit_bytes=60 * MIB
        ),
        name="relay_window",
    )(
        inflow[0], fresh[0], xz_weight[0].reshape(WIDTH, 2 * CHAN), proj_weight[0], out_weight[0],
        conv_weight[0], conv_bias, step_bias, decay_log, skip_weight, norm_gain,
    )
    return out[None]


def solution(mesh):
    placed = (
        P("section", "seq", None),
        P(None, "seq", None),
        P("section", None, None),
        P("section", None, None, "seq"),
        P("section", None, None),
        P("section", None),
        P("section", None),
        P("section", None),
        P("section", None),
        P("section", None),
        P("section", "seq", None),
    )
    return jax.shard_map(
        on_device,
        mesh=mesh,
        in_specs=placed,
        out_specs=P("section", None, "seq", None),
        check_vma=False,
    )
```

```python
import functools

import jax
import jax.numpy as jnp
from jax import lax
from jax.experimental import pallas as pl
from jax.experimental.pallas import tpu as pltpu
from jax.sharding import PartitionSpec as P

MESH = pl.DeviceIdType.MESH
F32 = jnp.float32
BF16 = jnp.bfloat16
HIGHEST = lax.Precision.HIGHEST
TOKENS = 1024
WIDTH = 4096
CHAN = 256
BLOCK = 128
BLOCKS = TOKENS // BLOCK
ROWS = 64
HALF = WIDTH // 2
COLS = 896
TILES = ((0, 256), (256, 256), (512, 256), (768, 128))
LAST = 7
PAD = 16
COPIES = 192
MIB = 2**20


def aligned(value, by):
    return pl.multiple_of(value, by)


def iota(shape, dim):
    return lax.broadcasted_iota(jnp.int32, shape, dim)


def columns(p):
    return pl.ds(p * HALF, HALF)


class Place:
    def __init__(self):
        self.sec = lax.axis_index("section")
        self.me = lax.axis_index("seq")
        self.z, self.h, self.c = self.me // 4, (self.me // 2) % 2, self.me % 2
        self.zp, self.zm, self.zz = (self.z + 1) % 4, (self.z + 3) % 4, (self.z + 2) % 4
        self.hh = 1 - self.h
        self.up = self.device(self.zp, self.h, self.c)
        self.down = self.device(self.zm, self.h, self.c)
        self.across = self.device(self.z, self.hh, self.c)
        self.sib = self.device(self.z, self.h, 1 - self.c)
        self.diag = self.device(self.z, self.hh, 1 - self.c)
        self.after = ((self.sec + 1) % 8, self.me)
        self.ahead = ((self.sec + 7) % 8, self.me)

    def device(self, z, h, c):
        return (self.sec, z * 4 + h * 2 + c)

    def meet(self):
        targets = [self.up, self.down, self.across, self.sib, self.diag, self.after, self.ahead]
        barrier = pltpu.get_barrier_semaphore()
        for target in targets:
            pl.semaphore_signal(barrier, inc=1, device_id=target, device_id_type=MESH)
        pl.semaphore_wait(barrier, len(targets))


class Copies:
    def __init__(self, send_sem, recv_sem):
        self.send_sem, self.recv_sem = send_sem, recv_sem
        self.count = 0
        self.open = []

    def make(self, src, dst, target):
        index = self.count
        self.count += 1
        return pltpu.make_async_remote_copy(
            src_ref=src,
            dst_ref=dst,
            send_sem=self.send_sem.at[index],
            recv_sem=self.recv_sem.at[index],
            device_id=target,
            device_id_type=MESH,
        )

    def new(self, src, dst, target):
        copy = self.make(src, dst, target)
        copy.start()
        self.open.append(copy)
        return copy

    def finish(self):
        for copy in self.open:
            copy.wait_send()
        self.open = []


class Gather:
    def __init__(self, at, copies, source, act, weight, acc, proj):
        self.at, self.copies, self.source = at, copies, source
        self.act, self.weight, self.acc, self.proj = act, weight, acc, proj
        self.got = {}

    def rows(self, z, h, p, half=None):
        start = (z * 2 + h) * 128 + self.at.c * ROWS
        if half is None:
            return self.act.at[pl.ds(aligned(start, ROWS), ROWS), columns(p)]
        return self.act.at[pl.ds(aligned(start + half * 32, 32), 32), columns(p)]

    def forward(self, z, h, p, target, half=None):
        return self.copies.new(self.rows(z, h, p, half), self.rows(z, h, p, half), target)

    def share(self, name, z, h, p, half=None):
        self.got.setdefault((name, p), []).append(self.forward(z, h, p, self.at.sib, half))

    def own(self, p):
        at = self.at
        src = self.source.at[:, columns(p)]
        dst = self.rows(at.z, at.h, p)
        for name, target in (("up", at.up), ("down", at.down), ("across", at.across), ("own", at.sib)):
            self.got[name, p] = [self.copies.new(src, dst, target)]

    def arrived(self, name, p):
        for copy in self.got[name, p]:
            copy.wait_recv()

    def near(self, p):
        at = self.at
        self.arrived("up", p)
        self.got["cu", p] = [self.forward(at.zm, at.h, p, at.up, 0)]
        self.arrived("down", p)
        self.got["cd", p] = [self.forward(at.zp, at.h, p, at.down, 1)]
        self.share("s_zm", at.zm, at.h, p)
        self.share("s_zp", at.zp, at.h, p)
        self.arrived("across", p)
        self.got["pu", p] = [self.forward(at.z, at.hh, p, at.up)]
        self.got["pd", p] = [self.forward(at.z, at.hh, p, at.down)]
        self.share("s_p", at.z, at.hh, p)

    def far(self, p):
        at = self.at
        for name, half in (("cu", 0), ("cd", 1)):
            self.arrived(name, p)
            self.got["cy%d" % half, p] = [self.forward(at.zz, at.h, p, at.across, half)]
            self.share("s_c", at.zz, at.h, p, half)

    def beside(self, p):
        at = self.at
        self.arrived("pu", p)
        self.share("s_pm", at.zm, at.hh, p)
        self.arrived("pd", p)
        self.share("s_pp", at.zp, at.hh, p)

    def last(self, p):
        at = self.at
        for half in (0, 1):
            self.arrived("cy%d" % half, p)
            self.share("s_cy", at.zz, at.hh, p, half)

    def project(self, name, z, h, p):
        self.arrived(name, p)
        start = (z * 2 + h) * 128
        at = pl.ds(aligned(start, 128), 128)
        padded = pl.ds(aligned(start + PAD, PAD), 128)
        for first, size in TILES:
            cols = pl.ds(first, size)
            part = jnp.dot(
                self.act[at, columns(p)], self.weight[columns(p), cols], preferred_element_type=F32
            )
            if p == 0:
                self.acc[at, cols] = part
            else:
                self.proj[padded, cols] = (self.acc[at, cols] + part).astype(BF16)

    def project_near(self, p):
        at = self.at
        self.project("own", at.z, at.h, p)
        self.project("s_zm", at.zm, at.h, p)
        self.project("s_zp", at.zp, at.h, p)
        self.project("s_p", at.z, at.hh, p)

    def project_beside(self, p):
        at = self.at
        self.project("s_pm", at.zm, at.hh, p)
        self.project("s_pp", at.zp, at.hh, p)

    def rest(self, mixer):
        at = self.at
        self.project_near(0)
        self.near(1)
        self.far(0)
        self.project_near(1)
        self.beside(0)
        self.project("s_c", at.zz, at.h, 0)
        self.far(1)
        mixer.local(0)
        self.project_beside(0)
        self.last(0)
        self.project("s_c", at.zz, at.h, 1)
        self.beside(1)
        self.project("s_cy", at.zz, at.hh, 0)
        self.project_beside(1)
        mixer.local(1)
        self.last(1)
        mixer.local(2)
        self.project("s_cy", at.zz, at.hh, 1)
        mixer.local(3)
        mixer.chain()


class Mixer:
    def __init__(self, at, params, proj, coded, sums, mixed, states, entering, window, gated, squares):
        self.proj, self.coded, self.sums, self.mixed = proj, coded, sums, mixed
        self.states, self.entering, self.window = states, entering, window
        self.gated, self.squares = gated, squares
        conv_w, conv_b, step_b, decay, skip, gain = params
        group = at.me // 4
        x_at = aligned(at.me * CHAN, CHAN)
        b_at = aligned(4096 + (group // 2) * 128, 128)
        c_at = aligned(4352 + (group // 2) * 128, 128)

        def own(ref):
            return jnp.concatenate(
                [ref[:, pl.ds(x_at, CHAN)], ref[:, pl.ds(b_at, 128)], ref[:, pl.ds(c_at, 128)]], axis=1
            )

        spread = (iota((128, CHAN), 0) == at.me * 8 + iota((128, CHAN), 1) // 32).astype(F32)

        def per_channel(ref):
            wide = jnp.broadcast_to(ref[...], (8, 128))
            return jnp.dot(wide, spread, precision=HIGHEST, preferred_element_type=F32)[0:1]

        self.taps, self.offset = own(conv_w), own(conv_b)
        self.bias = per_channel(step_b)
        self.rate = -jnp.exp(per_channel(decay))
        self.direct = per_channel(skip)
        self.gains = gain[:, pl.ds(x_at, CHAN)]
        self.spread = spread.astype(BF16)
        self.half = group % 2
        one, two = at.hh, at.h
        self.order = [
            one * (2 * at.z + 1) + two * (2 * at.z),
            one * (2 * at.zp) + two * (2 * at.z + 1),
            one * (2 * at.z) + two * (2 * at.zp),
            one * (2 * at.zm + 1) + two * (2 * at.zp + 1),
            one * (2 * at.zp + 1) + two * (2 * at.zm),
            one * (2 * at.zz) + two * (2 * at.zm + 1),
            one * (2 * at.zm) + two * (2 * at.zz),
            2 * at.zz + 1,
        ]
        proj[0:PAD, :] = jnp.zeros((PAD, COLS), BF16)

    def local(self, pair):
        first, second = self.order[2 * pair], self.order[2 * pair + 1]
        taps, window = self.taps, self.window
        lower = iota((BLOCK, BLOCK), 0) >= iota((BLOCK, BLOCK), 1)
        lower_ones = lower.astype(F32)
        own_half = iota((BLOCK, 128), 1) // 64 == self.half
        head_of = iota((BLOCK, CHAN), 1) // 32

        def block(index, carry):
            start = ((1 - index) * first + index * second) * BLOCK
            at = pl.ds(aligned(start, BLOCK), BLOCK)
            rows = pl.ds(aligned(start + PAD, PAD), BLOCK)
            window[0:PAD, :] = self.proj[pl.ds(aligned(start, PAD), PAD), pl.ds(256, 512)].astype(F32)
            window[PAD : PAD + BLOCK, :] = self.proj[rows, pl.ds(256, 512)].astype(F32)
            conv = self.offset + taps[0:1] * window[PAD - 3 : PAD - 3 + BLOCK, :]
            for k in range(1, 4):
                conv = conv + taps[k : k + 1] * window[PAD - 3 + k : PAD - 3 + k + BLOCK, :]
            conv = (conv / (1.0 + jnp.exp(-conv))).astype(BF16)
            x = conv[:, :CHAN]
            b = conv[:, CHAN : CHAN + 128]
            c = jnp.where(own_half, conv[:, CHAN + 128 :], jnp.zeros((), BF16))
            self.coded[at, :] = c
            step = jax.nn.softplus(
                jnp.dot(self.proj[rows, pl.ds(768, 128)], self.spread, preferred_element_type=F32)
                + self.bias
            )
            cumulus = jnp.dot(
                lower_ones, self.rate * step, precision=HIGHEST, preferred_element_type=F32
            )
            self.sums[at, :] = cumulus
            cumulus_t = cumulus.T
            step_t = step.T
            scores = lax.dot_general(c, b, (((1,), (1,)), ((), ())), preferred_element_type=F32)
            mixing, values = [], []
            for head in range(8):
                lane = 32 * head
                gap = cumulus[:, lane : lane + 1] - cumulus_t[lane : lane + 1, :]
                gap = jnp.where(lower, gap, -1e30)
                mixing.append((scores * jnp.exp(gap) * step_t[lane : lane + 1, :]).astype(BF16))
                values.append(jnp.where(head_of == head, x, jnp.zeros((), BF16)))
            diagonal = jnp.dot(
                jnp.concatenate(mixing, axis=1),
                jnp.concatenate(values, axis=0),
                preferred_element_type=F32,
            )
            x32 = x.astype(F32)
            self.mixed[at, :] = diagonal + self.direct * x32
            total = cumulus[BLOCK - 1 : BLOCK]
            weighted = (x32 * (jnp.exp(total - cumulus) * step)).astype(BF16)
            self.states[at, :] = lax.dot_general(
                b, weighted, (((0,), (0,)), ((), ())), preferred_element_type=F32
            )
            return carry

        lax.fori_loop(0, 2, block, 0)

    def chain(self):
        state = jnp.zeros((BLOCK, CHAN), F32)
        for index in range(BLOCKS):
            at = pl.ds(index * BLOCK, BLOCK)
            self.entering[at, :] = state.astype(BF16)
            if index < BLOCKS - 1:
                total = self.sums[(index + 1) * BLOCK - 1 : (index + 1) * BLOCK, :]
                state = jnp.exp(total) * state + self.states[at, :]

    def outputs(self, z):
        def block(index, carry):
            start = z * 256 + index * BLOCK
            at = pl.ds(aligned(start, BLOCK), BLOCK)
            mixed = self.mixed[at, :] + jnp.exp(self.sums[at, :]) * jnp.dot(
                self.coded[at, :], self.entering[at, :], preferred_element_type=F32
            )
            gate = self.proj[pl.ds(aligned(start + PAD, PAD), BLOCK), pl.ds(0, CHAN)].astype(F32)
            gated = mixed * (gate / (1.0 + jnp.exp(-gate)))
            self.squares[:, at] = lax.dot_general(
                jnp.ones((8, CHAN), F32),
                gated * gated,
                (((1,), (1,)), ((), ())),
                precision=HIGHEST,
                preferred_element_type=F32,
            )
            self.gated[at, :] = (gated * self.gains).astype(BF16)
            return carry

        lax.fori_loop(0, 2, block, 0)


class Scatter:
    def __init__(self, at, copies, mixer, wout, part, from_sib, got, stats, scale):
        self.at, self.copies, self.mixer, self.wout = at, copies, mixer, wout
        self.part, self.from_sib, self.got, self.stats, self.scale = part, from_sib, got, stats, scale
        self.sent = {}

    def gate(self, z):
        self.mixer.outputs(z)
        cols = pl.ds(aligned(z * 256, 256), 256)
        squares = self.mixer.squares.at[:, cols]
        self.shares = [
            self.copies.new(squares, self.stats.at[i, :, cols], target)
            for i, target in enumerate((self.at.sib, self.at.across, self.at.diag))
        ]
        return z, self.shares

    def factor(self, gate):
        z, shares = gate
        for share in shares:
            share.wait_recv()
        for i in (0, 1):
            at = pl.ds(aligned(z * 256 + i * 128, 128), 128)
            total = self.mixer.squares[:, at] + self.stats[0, :, at]
            total = total + self.stats[1, :, at] + self.stats[2, :, at]
            self.scale[at, :] = lax.dot_general(
                lax.rsqrt(total / 1024.0 + 1e-05),
                jnp.full((8, 128), 0.125, F32),
                (((0,), (0,)), ((), ())),
                precision=HIGHEST,
                preferred_element_type=F32,
            )

    def mine(self, z, h, p, half=None):
        start = (z * 2 + h) * 128 + self.at.c * ROWS
        if half is None:
            return self.part.at[pl.ds(aligned(start, ROWS), ROWS), columns(p)]
        return self.part.at[pl.ds(aligned(start + half * 32, 32), 32), columns(p)]

    def compute(self, z, h, p):
        start = aligned((z * 2 + h) * 128, 128)
        at = pl.ds(start, 128)
        lhs = self.mixer.gated[at, :]

        def tile(n, carry):
            cols = pl.ds(aligned(p * HALF + n * 512, 512), 512)
            self.part[at, cols] = jnp.dot(
                lhs, self.wout[:, cols], preferred_element_type=F32
            ).astype(BF16)
            return carry

        lax.fori_loop(0, HALF // 512, tile, 0)
        src = self.part.at[pl.ds(aligned(start + (1 - self.at.c) * ROWS, ROWS), ROWS), columns(p)]
        dst = self.from_sib.at[pl.ds(aligned((z * 2 + h) * ROWS, ROWS), ROWS), columns(p)]
        return self.copies.new(src, dst, self.at.sib)

    def pair(self, z, h, p, copy):
        copy.wait_recv()
        own = self.mine(z, h, p)
        other = self.from_sib.at[pl.ds(aligned((z * 2 + h) * ROWS, ROWS), ROWS), columns(p)]
        rows = pl.ds(aligned((z * 2 + h) * 128 + self.at.c * ROWS, ROWS), ROWS)
        scale = jnp.concatenate([self.scale[rows, :]] * 2, axis=1)

        def tile(n, carry):
            cols = pl.ds(aligned(n * 256, 256), 256)
            total = own[:, cols].astype(F32) + other[:, cols].astype(F32)
            own[:, cols] = (total * scale).astype(BF16)
            return carry

        lax.fori_loop(0, HALF // 256, tile, 0)

    @staticmethod
    def add(dst, *others):
        def tile(n, carry):
            cols = pl.ds(aligned(n * 256, 256), 256)
            total = dst[:, cols].astype(F32)
            for other in others:
                total = total + other[:, cols].astype(F32)
            dst[:, cols] = total.astype(BF16)
            return carry

        lax.fori_loop(0, HALF // 256, tile, 0)

    def send(self, name, src, slot, p, target, half=None):
        dst = self.got.at[p, slot]
        if half is not None:
            dst = self.got.at[p, slot, pl.ds(half * 32, 32)]
        self.sent.setdefault((name, p), []).append(self.copies.new(src, dst, target))

    def arrived(self, name, p):
        for copy in self.sent[name, p]:
            copy.wait_recv()

    def first(self):
        at = self.at
        g_zz = self.gate(at.zz)
        g_zp = self.gate(at.zp)
        c_zzhh = self.compute(at.zz, at.hh, 0)
        g_zm = self.gate(at.zm)
        c_zphh = self.compute(at.zp, at.hh, 0)
        g_z = self.gate(at.z)
        c_zmhh = self.compute(at.zm, at.hh, 0)
        self.factor(g_zz)
        self.pair(at.zz, at.hh, 0, c_zzhh)
        self.send("y1", self.mine(at.zz, at.hh, 0), 0, 0, at.across)
        self.factor(g_zp)
        self.pair(at.zp, at.hh, 0, c_zphh)
        self.send("u5", self.mine(at.zp, at.hh, 0), 1, 0, at.up)
        self.factor(g_zm)
        self.pair(at.zm, at.hh, 0, c_zmhh)
        self.send("d5", self.mine(at.zm, at.hh, 0), 2, 0, at.down)
        c_zzh = self.compute(at.zz, at.h, 0)
        c_zph = self.compute(at.zp, at.h, 0)
        c_zmh = self.compute(at.zm, at.h, 0)
        self.pair(at.zz, at.h, 0, c_zzh)
        self.pair(at.zp, at.h, 0, c_zph)
        self.send("u4", self.mine(at.zp, at.h, 0, 0), 3, 0, at.up, 0)
        self.pair(at.zm, at.h, 0, c_zmh)
        self.send("d4", self.mine(at.zm, at.h, 0, 1), 4, 0, at.down, 1)
        c_zhh = self.compute(at.z, at.hh, 0)
        c_zh = self.compute(at.z, at.h, 0)
        self.factor(g_z)
        self.pair(at.z, at.hh, 0, c_zhh)
        self.pair(at.z, at.h, 0, c_zh)

    def second(self):
        at = self.at
        c_zzhh = self.compute(at.zz, at.hh, 1)
        c_zphh = self.compute(at.zp, at.hh, 1)
        self.pair(at.zz, at.hh, 1, c_zzhh)
        self.send("y1", self.mine(at.zz, at.hh, 1), 0, 1, at.across)
        c_zmhh = self.compute(at.zm, at.hh, 1)
        self.pair(at.zp, at.hh, 1, c_zphh)
        self.send("u5", self.mine(at.zp, at.hh, 1), 1, 1, at.up)
        self.pair(at.zm, at.hh, 1, c_zmhh)
        self.send("d5", self.mine(at.zm, at.hh, 1), 2, 1, at.down)
        c_zzh = self.compute(at.zz, at.h, 1)
        self.cross(0)
        c_zph = self.compute(at.zp, at.h, 1)
        c_zmh = self.compute(at.zm, at.h, 1)
        self.pair(at.zz, at.h, 1, c_zzh)
        self.side(0)
        self.pair(at.zp, at.h, 1, c_zph)
        self.send("u4", self.mine(at.zp, at.h, 1, 0), 3, 1, at.up, 0)
        self.pair(at.zm, at.h, 1, c_zmh)
        self.send("d4", self.mine(at.zm, at.h, 1, 1), 4, 1, at.down, 1)
        c_zhh = self.compute(at.z, at.hh, 1)
        c_zh = self.compute(at.z, at.h, 1)
        self.join(0)
        self.pair(at.z, at.hh, 1, c_zhh)
        self.pair(at.z, at.h, 1, c_zh)
        self.cross(1)
        self.side(1)

    def cross(self, p):
        at = self.at
        self.arrived("y1", p)
        self.add(self.mine(at.zz, at.h, p), self.got.at[p, 0])
        self.send("c_down", self.mine(at.zz, at.h, p, 0), 5, p, at.down, 0)
        self.send("c_up", self.mine(at.zz, at.h, p, 1), 5, p, at.up, 1)

    def side(self, p):
        at = self.at
        self.arrived("u5", p)
        self.arrived("d5", p)
        self.add(self.mine(at.z, at.hh, p), self.got.at[p, 1], self.got.at[p, 2])
        self.send("y6", self.mine(at.z, at.hh, p), 6, p, at.across)

    def join(self, p):
        at = self.at
        self.arrived("c_down", p)
        self.add(self.mine(at.zm, at.h, p, 0), self.got.at[p, 5, pl.ds(0, 32)])
        self.send("d4", self.mine(at.zm, at.h, p, 0), 4, p, at.down, 0)
        self.arrived("c_up", p)
        self.add(self.mine(at.zp, at.h, p, 1), self.got.at[p, 5, pl.ds(32, 32)])
        self.send("u4", self.mine(at.zp, at.h, p, 1), 3, p, at.up, 1)

    def total(self, p, out, staged):
        at = self.at
        for name in ("y6", "u4", "d4"):
            self.arrived(name, p)
        own = self.mine(at.z, at.h, p)

        def tile(n, carry):
            cols = pl.ds(aligned(n * 256, 256), 256)
            wide = pl.ds(aligned(p * HALF + n * 256, 256), 256)
            total = own[:, cols].astype(F32) + self.got[p, 6, :, cols].astype(F32)
            total = total + self.got[p, 3, :, cols].astype(F32) + self.got[p, 4, :, cols].astype(F32)
            out[:, wide] = total
            if staged is not None:
                staged[:, wide] = total.astype(BF16)
            return carry

        lax.fori_loop(0, HALF // 256, tile, 0)


def kernel(
    inflow, fresh, wxz, wproj, wout, conv_w, conv_b, step_b, decay, skip, gain, out,
    act, weight, acc, proj, coded, sums, mixed, states, entering, window, gated, squares,
    part, from_sib, got, stats, scale, staged, received, send_sem, recv_sem, local_sem,
):
    at = Place()
    pair = at.z // 2
    here = pl.ds(aligned(at.me * ROWS, ROWS), ROWS)
    loads = []
    for index, (src, dst) in enumerate(
        [
            (inflow, act.at[here]),
            (wxz, weight.at[:, pl.ds(0, 2 * CHAN)]),
            (wproj.at[:, pl.ds(aligned(pair * 128, 128), 128)], weight.at[:, pl.ds(512, 128)]),
            (wproj.at[:, pl.ds(aligned(256 + pair * 128, 128), 128)], weight.at[:, pl.ds(640, 128)]),
            (wproj.at[:, pl.ds(512, 128)], weight.at[:, pl.ds(768, 128)]),
        ]
    ):
        load = pltpu.make_async_copy(src, dst, local_sem.at[index])
        load.start()
        loads.append(load)
    at.meet()
    copies = Copies(send_sem, recv_sem)
    mixer = Mixer(
        at, (conv_w, conv_b, step_b, decay, skip, gain),
        proj, coded, sums, mixed, states, entering, window, gated, squares,
    )
    scatter_refs = (wout, part, from_sib, got, stats, scale)

    gather = Gather(at, copies, inflow, act, weight, acc, proj)
    gather.own(0)
    gather.own(1)
    gather.near(0)
    for load in loads:
        load.wait()

    @pl.when(at.sec == 0)
    def _():
        load = pltpu.make_async_copy(fresh, received, local_sem.at[0])
        load.start()
        load.wait()

    gather.rest(mixer)
    copies.finish()

    scatter = Scatter(at, copies, mixer, *scatter_refs)
    hops = [copies.make(staged.at[:, columns(p)], received.at[:, columns(p)], at.after) for p in (0, 1)]

    def relay(p):
        scatter.total(p, out.at[0], staged)
        pl.when(at.sec < LAST)(hops[p].start)

    def relayed(p):
        pl.when(at.sec > 0)(hops[p].wait_recv)
        keep = pltpu.make_async_copy(
            received.at[:, columns(p)], act.at[here, columns(p)], local_sem.at[p]
        )
        keep.start()
        gather.own(p)
        return keep

    scatter.first()
    scatter.second()
    relay(0)
    scatter.join(1)
    gather = Gather(at, copies, received, act, weight, acc, proj)
    keeps = [relayed(0)]
    relay(1)
    gather.near(0)
    keeps.append(relayed(1))
    for keep in keeps:
        keep.wait()
    gather.rest(mixer)
    for p in (0, 1):
        pl.when(at.sec < LAST)(hops[p].wait_send)
    copies.finish()

    scatter = Scatter(at, copies, mixer, *scatter_refs)
    scatter.first()
    scatter.second()
    scatter.join(1)
    scatter.total(0, out.at[1], None)
    scatter.total(1, out.at[1], None)
    copies.finish()


def on_device(
    inflow,
    fresh,
    proj_weight,
    xz_weight,
    conv_weight,
    conv_bias,
    step_bias,
    decay_log,
    skip_weight,
    norm_gain,
    out_weight,
):
    anywhere = pl.BlockSpec(memory_space=pl.ANY)
    vmem = pl.BlockSpec(memory_space=pltpu.VMEM)
    out = pl.pallas_call(
        kernel,
        out_shape=jax.ShapeDtypeStruct((2, ROWS, WIDTH), F32),
        in_specs=[anywhere] * 4 + [vmem] * 7,
        out_specs=vmem,
        scratch_shapes=[
            pltpu.VMEM((TOKENS, WIDTH), BF16),
            pltpu.VMEM((WIDTH, COLS), BF16),
            pltpu.VMEM((TOKENS, COLS), F32),
            pltpu.VMEM((TOKENS + PAD, COLS), BF16),
            pltpu.VMEM((TOKENS, 128), BF16),
            pltpu.VMEM((TOKENS, CHAN), F32),
            pltpu.VMEM((TOKENS, CHAN), F32),
            pltpu.VMEM((TOKENS, CHAN), F32),
            pltpu.VMEM((TOKENS, CHAN), BF16),
            pltpu.VMEM((BLOCK + PAD, 512), F32),
            pltpu.VMEM((TOKENS, CHAN), BF16),
            pltpu.VMEM((8, TOKENS), F32),
            pltpu.VMEM((TOKENS, WIDTH), BF16),
            pltpu.VMEM((TOKENS // 2, WIDTH), BF16),
            pltpu.VMEM((2, LAST, ROWS, HALF), BF16),
            pltpu.VMEM((3, 8, TOKENS), F32),
            pltpu.VMEM((TOKENS, 128), F32),
            pltpu.VMEM((ROWS, WIDTH), BF16),
            pltpu.VMEM((ROWS, WIDTH), BF16),
            pltpu.SemaphoreType.DMA((COPIES,)),
            pltpu.SemaphoreType.DMA((COPIES,)),
            pltpu.SemaphoreType.DMA((5,)),
        ],
        compiler_params=pltpu.CompilerParams(
            collective_id=0, has_side_effects=True, vmem_limit_bytes=60 * MIB
        ),
        name="relay_window",
    )(
        inflow[0], fresh[0], xz_weight[0].reshape(WIDTH, 2 * CHAN), proj_weight[0], out_weight[0],
        conv_weight[0], conv_bias, step_bias, decay_log, skip_weight, norm_gain,
    )
    return out[None]


def solution(mesh):
    placed = (
        P("section", "seq", None),
        P(None, "seq", None),
        P("section", None, None),
        P("section", None, None, "seq"),
        P("section", None, None),
        P("section", None),
        P("section", None),
        P("section", None),
        P("section", None),
        P("section", None),
        P("section", "seq", None),
    )
    return jax.shard_map(
        on_device,
        mesh=mesh,
        in_specs=placed,
        out_specs=P("section", None, "seq", None),
        check_vma=False,
    )
```

```python
import functools

import jax
import jax.numpy as jnp
from jax import lax
from jax.experimental import pallas as pl
from jax.experimental.pallas import tpu as pltpu
from jax.sharding import PartitionSpec as P

MESH = pl.DeviceIdType.MESH
F32 = jnp.float32
BF16 = jnp.bfloat16
HIGHEST = lax.Precision.HIGHEST
TOKENS = 1024
WIDTH = 4096
CHAN = 256
BLOCK = 128
BLOCKS = TOKENS // BLOCK
ROWS = 64
HALF = WIDTH // 2
COLS = 896
TILES = ((0, 256), (256, 256), (512, 256), (768, 128))
LAST = 7
PAD = 16
COPIES = 192
MIB = 2**20


def aligned(value, by):
    return pl.multiple_of(value, by)


def iota(shape, dim):
    return lax.broadcasted_iota(jnp.int32, shape, dim)


def columns(p):
    return pl.ds(p * HALF, HALF)


class Place:
    def __init__(self):
        self.sec = lax.axis_index("section")
        self.me = lax.axis_index("seq")
        self.z, self.h, self.c = self.me // 4, (self.me // 2) % 2, self.me % 2
        self.zp, self.zm, self.zz = (self.z + 1) % 4, (self.z + 3) % 4, (self.z + 2) % 4
        self.hh = 1 - self.h
        self.up = self.device(self.zp, self.h, self.c)
        self.down = self.device(self.zm, self.h, self.c)
        self.across = self.device(self.z, self.hh, self.c)
        self.sib = self.device(self.z, self.h, 1 - self.c)
        self.diag = self.device(self.z, self.hh, 1 - self.c)
        self.after = ((self.sec + 1) % 8, self.me)
        self.ahead = ((self.sec + 7) % 8, self.me)

    def device(self, z, h, c):
        return (self.sec, z * 4 + h * 2 + c)

    def meet(self):
        targets = [self.up, self.down, self.across, self.sib, self.diag, self.after, self.ahead]
        barrier = pltpu.get_barrier_semaphore()
        for target in targets:
            pl.semaphore_signal(barrier, inc=1, device_id=target, device_id_type=MESH)
        pl.semaphore_wait(barrier, len(targets))


class Copies:
    def __init__(self, send_sem, recv_sem):
        self.send_sem, self.recv_sem = send_sem, recv_sem
        self.count = 0
        self.open = []

    def make(self, src, dst, target):
        index = self.count
        self.count += 1
        return pltpu.make_async_remote_copy(
            src_ref=src,
            dst_ref=dst,
            send_sem=self.send_sem.at[index],
            recv_sem=self.recv_sem.at[index],
            device_id=target,
            device_id_type=MESH,
        )

    def new(self, src, dst, target):
        copy = self.make(src, dst, target)
        copy.start()
        self.open.append(copy)
        return copy

    def finish(self):
        for copy in self.open:
            copy.wait_send()
        self.open = []


class Gather:
    def __init__(self, at, copies, source, act, weight, acc, proj):
        self.at, self.copies, self.source = at, copies, source
        self.act, self.weight, self.acc, self.proj = act, weight, acc, proj
        self.got = {}

    def rows(self, z, h, p, half=None):
        start = (z * 2 + h) * 128 + self.at.c * ROWS
        if half is None:
            return self.act.at[pl.ds(aligned(start, ROWS), ROWS), columns(p)]
        return self.act.at[pl.ds(aligned(start + half * 32, 32), 32), columns(p)]

    def forward(self, z, h, p, target, half=None):
        return self.copies.new(self.rows(z, h, p, half), self.rows(z, h, p, half), target)

    def share(self, name, z, h, p, half=None):
        self.got.setdefault((name, p), []).append(self.forward(z, h, p, self.at.sib, half))

    def own(self, p):
        at = self.at
        src = self.source.at[:, columns(p)]
        dst = self.rows(at.z, at.h, p)
        for name, target in (("up", at.up), ("down", at.down), ("across", at.across), ("own", at.sib)):
            self.got[name, p] = [self.copies.new(src, dst, target)]

    def arrived(self, name, p):
        for copy in self.got[name, p]:
            copy.wait_recv()

    def near(self, p):
        at = self.at
        self.arrived("up", p)
        self.got["cu", p] = [self.forward(at.zm, at.h, p, at.up, 0)]
        self.arrived("down", p)
        self.got["cd", p] = [self.forward(at.zp, at.h, p, at.down, 1)]
        self.share("s_zm", at.zm, at.h, p)
        self.share("s_zp", at.zp, at.h, p)
        self.arrived("across", p)
        self.got["pu", p] = [self.forward(at.z, at.hh, p, at.up)]
        self.got["pd", p] = [self.forward(at.z, at.hh, p, at.down)]
        self.share("s_p", at.z, at.hh, p)

    def far(self, p):
        at = self.at
        for name, half in (("cu", 0), ("cd", 1)):
            self.arrived(name, p)
            self.got["cy%d" % half, p] = [self.forward(at.zz, at.h, p, at.across, half)]
            self.share("s_c", at.zz, at.h, p, half)

    def beside(self, p):
        at = self.at
        self.arrived("pu", p)
        self.share("s_pm", at.zm, at.hh, p)
        self.arrived("pd", p)
        self.share("s_pp", at.zp, at.hh, p)

    def last(self, p):
        at = self.at
        for half in (0, 1):
            self.arrived("cy%d" % half, p)
            self.share("s_cy", at.zz, at.hh, p, half)

    def project(self, name, z, h, p):
        self.arrived(name, p)
        start = (z * 2 + h) * 128
        at = pl.ds(aligned(start, 128), 128)
        padded = pl.ds(aligned(start + PAD, PAD), 128)
        for first, size in TILES:
            cols = pl.ds(first, size)
            part = jnp.dot(
                self.act[at, columns(p)], self.weight[columns(p), cols], preferred_element_type=F32
            )
            if p == 0:
                self.acc[at, cols] = part
            else:
                self.proj[padded, cols] = (self.acc[at, cols] + part).astype(BF16)

    def project_near(self, p):
        at = self.at
        self.project("own", at.z, at.h, p)
        self.project("s_zm", at.zm, at.h, p)
        self.project("s_zp", at.zp, at.h, p)
        self.project("s_p", at.z, at.hh, p)

    def project_beside(self, p):
        at = self.at
        self.project("s_pm", at.zm, at.hh, p)
        self.project("s_pp", at.zp, at.hh, p)

    def rest(self, mixer):
        at = self.at
        self.project_near(0)
        self.near(1)
        self.far(0)
        self.project_near(1)
        self.beside(0)
        self.project("s_c", at.zz, at.h, 0)
        self.far(1)
        mixer.local(0)
        self.project_beside(0)
        self.last(0)
        self.project("s_c", at.zz, at.h, 1)
        self.beside(1)
        self.project("s_cy", at.zz, at.hh, 0)
        self.project_beside(1)
        mixer.local(1)
        self.last(1)
        mixer.local(2)
        self.project("s_cy", at.zz, at.hh, 1)
        mixer.local(3)
        mixer.chain()


class Mixer:
    def __init__(self, at, params, proj, coded, sums, mixed, states, entering, window, gated, squares):
        self.proj, self.coded, self.sums, self.mixed = proj, coded, sums, mixed
        self.states, self.entering, self.window = states, entering, window
        self.gated, self.squares = gated, squares
        conv_w, conv_b, step_b, decay, skip, gain = params
        group = at.me // 4
        x_at = aligned(at.me * CHAN, CHAN)
        b_at = aligned(4096 + (group // 2) * 128, 128)
        c_at = aligned(4352 + (group // 2) * 128, 128)

        def own(ref):
            return jnp.concatenate(
                [ref[:, pl.ds(x_at, CHAN)], ref[:, pl.ds(b_at, 128)], ref[:, pl.ds(c_at, 128)]], axis=1
            )

        spread = (iota((128, CHAN), 0) == at.me * 8 + iota((128, CHAN), 1) // 32).astype(F32)

        def per_channel(ref):
            wide = jnp.broadcast_to(ref[...], (8, 128))
            return jnp.dot(wide, spread, precision=HIGHEST, preferred_element_type=F32)[0:1]

        self.taps, self.offset = own(conv_w), own(conv_b)
        self.bias = per_channel(step_b)
        self.rate = -jnp.exp(per_channel(decay))
        self.direct = per_channel(skip)
        self.gains = gain[:, pl.ds(x_at, CHAN)]
        self.spread = spread.astype(BF16)
        self.half = group % 2
        one, two = at.hh, at.h
        self.order = [
            one * (2 * at.z + 1) + two * (2 * at.z),
            one * (2 * at.zp) + two * (2 * at.z + 1),
            one * (2 * at.z) + two * (2 * at.zp),
            one * (2 * at.zm + 1) + two * (2 * at.zp + 1),
            one * (2 * at.zp + 1) + two * (2 * at.zm),
            one * (2 * at.zz) + two * (2 * at.zm + 1),
            one * (2 * at.zm) + two * (2 * at.zz),
            2 * at.zz + 1,
        ]
        proj[0:PAD, :] = jnp.zeros((PAD, COLS), BF16)

    def local(self, pair):
        first, second = self.order[2 * pair], self.order[2 * pair + 1]
        taps, window = self.taps, self.window
        lower = iota((BLOCK, BLOCK), 0) >= iota((BLOCK, BLOCK), 1)
        lower_ones = lower.astype(F32)
        own_half = iota((BLOCK, 128), 1) // 64 == self.half
        head_of = iota((BLOCK, CHAN), 1) // 32

        def block(index, carry):
            start = ((1 - index) * first + index * second) * BLOCK
            at = pl.ds(aligned(start, BLOCK), BLOCK)
            rows = pl.ds(aligned(start + PAD, PAD), BLOCK)
            window[0:PAD, :] = self.proj[pl.ds(aligned(start, PAD), PAD), pl.ds(256, 512)].astype(F32)
            window[PAD : PAD + BLOCK, :] = self.proj[rows, pl.ds(256, 512)].astype(F32)
            conv = self.offset + taps[0:1] * window[PAD - 3 : PAD - 3 + BLOCK, :]
            for k in range(1, 4):
                conv = conv + taps[k : k + 1] * window[PAD - 3 + k : PAD - 3 + k + BLOCK, :]
            conv = (conv / (1.0 + jnp.exp(-conv))).astype(BF16)
            x = conv[:, :CHAN]
            b = conv[:, CHAN : CHAN + 128]
            c = jnp.where(own_half, conv[:, CHAN + 128 :], jnp.zeros((), BF16))
            self.coded[at, :] = c
            step = jax.nn.softplus(
                jnp.dot(self.proj[rows, pl.ds(768, 128)], self.spread, preferred_element_type=F32)
                + self.bias
            )
            cumulus = jnp.dot(
                lower_ones, self.rate * step, precision=HIGHEST, preferred_element_type=F32
            )
            self.sums[at, :] = cumulus
            cumulus_t = cumulus.T
            step_t = step.T
            scores = lax.dot_general(c, b, (((1,), (1,)), ((), ())), preferred_element_type=F32)
            mixing, values = [], []
            for head in range(8):
                lane = 32 * head
                gap = cumulus[:, lane : lane + 1] - cumulus_t[lane : lane + 1, :]
                gap = jnp.where(lower, gap, -1e30)
                mixing.append((scores * jnp.exp(gap) * step_t[lane : lane + 1, :]).astype(BF16))
                values.append(jnp.where(head_of == head, x, jnp.zeros((), BF16)))
            diagonal = jnp.dot(
                jnp.concatenate(mixing, axis=1),
                jnp.concatenate(values, axis=0),
                preferred_element_type=F32,
            )
            x32 = x.astype(F32)
            self.mixed[at, :] = diagonal + self.direct * x32
            total = cumulus[BLOCK - 1 : BLOCK]
            weighted = (x32 * (jnp.exp(total - cumulus) * step)).astype(BF16)
            self.states[at, :] = lax.dot_general(
                b, weighted, (((0,), (0,)), ((), ())), preferred_element_type=F32
            )
            return carry

        lax.fori_loop(0, 2, block, 0)

    def chain(self):
        state = jnp.zeros((BLOCK, CHAN), F32)
        for index in range(BLOCKS):
            at = pl.ds(index * BLOCK, BLOCK)
            self.entering[at, :] = state.astype(BF16)
            if index < BLOCKS - 1:
                total = self.sums[(index + 1) * BLOCK - 1 : (index + 1) * BLOCK, :]
                state = jnp.exp(total) * state + self.states[at, :]

    def outputs(self, z):
        def block(index, carry):
            start = z * 256 + index * BLOCK
            at = pl.ds(aligned(start, BLOCK), BLOCK)
            mixed = self.mixed[at, :] + jnp.exp(self.sums[at, :]) * jnp.dot(
                self.coded[at, :], self.entering[at, :], preferred_element_type=F32
            )
            gate = self.proj[pl.ds(aligned(start + PAD, PAD), BLOCK), pl.ds(0, CHAN)].astype(F32)
            gated = mixed * (gate / (1.0 + jnp.exp(-gate)))
            self.squares[:, at] = lax.dot_general(
                jnp.ones((8, CHAN), F32),
                gated * gated,
                (((1,), (1,)), ((), ())),
                precision=HIGHEST,
                preferred_element_type=F32,
            )
            self.gated[at, :] = (gated * self.gains).astype(BF16)
            return carry

        lax.fori_loop(0, 2, block, 0)


class Scatter:
    def __init__(self, at, copies, mixer, wout, part, from_sib, got, stats, scale):
        self.at, self.copies, self.mixer, self.wout = at, copies, mixer, wout
        self.part, self.from_sib, self.got, self.stats, self.scale = part, from_sib, got, stats, scale
        self.sent = {}

    def gate(self, z):
        self.mixer.outputs(z)
        cols = pl.ds(aligned(z * 256, 256), 256)
        squares = self.mixer.squares.at[:, cols]
        self.shares = [
            self.copies.new(squares, self.stats.at[i, :, cols], target)
            for i, target in enumerate((self.at.sib, self.at.across, self.at.diag))
        ]
        return z, self.shares

    def factor(self, gate):
        z, shares = gate
        for share in shares:
            share.wait_recv()
        for i in (0, 1):
            at = pl.ds(aligned(z * 256 + i * 128, 128), 128)
            total = self.mixer.squares[:, at] + self.stats[0, :, at]
            total = total + self.stats[1, :, at] + self.stats[2, :, at]
            self.scale[at, :] = lax.dot_general(
                lax.rsqrt(total / 1024.0 + 1e-05),
                jnp.full((8, 128), 0.125, F32),
                (((0,), (0,)), ((), ())),
                precision=HIGHEST,
                preferred_element_type=F32,
            )

    def mine(self, z, h, p, half=None):
        start = (z * 2 + h) * 128 + self.at.c * ROWS
        if half is None:
            return self.part.at[pl.ds(aligned(start, ROWS), ROWS), columns(p)]
        return self.part.at[pl.ds(aligned(start + half * 32, 32), 32), columns(p)]

    def compute(self, z, p):
        at = pl.ds(aligned(z * 256, 256), 256)
        lhs = self.mixer.gated[at, :]

        def tile(n, carry):
            cols = pl.ds(aligned(p * HALF + n * 512, 512), 512)
            self.part[at, cols] = jnp.dot(
                lhs, self.wout[:, cols], preferred_element_type=F32
            ).astype(BF16)
            return carry

        lax.fori_loop(0, HALF // 512, tile, 0)
        copies = []
        for h in (self.at.hh, self.at.h):
            start = (z * 2 + h) * 128 + (1 - self.at.c) * ROWS
            src = self.part.at[pl.ds(aligned(start, ROWS), ROWS), columns(p)]
            dst = self.from_sib.at[pl.ds(aligned((z * 2 + h) * ROWS, ROWS), ROWS), columns(p)]
            copies.append(self.copies.new(src, dst, self.at.sib))
        return copies

    def pair(self, z, h, p, copy):
        copy.wait_recv()
        own = self.mine(z, h, p)
        other = self.from_sib.at[pl.ds(aligned((z * 2 + h) * ROWS, ROWS), ROWS), columns(p)]
        rows = pl.ds(aligned((z * 2 + h) * 128 + self.at.c * ROWS, ROWS), ROWS)
        scale = jnp.concatenate([self.scale[rows, :]] * 2, axis=1)

        def tile(n, carry):
            cols = pl.ds(aligned(n * 256, 256), 256)
            total = own[:, cols].astype(F32) + other[:, cols].astype(F32)
            own[:, cols] = (total * scale).astype(BF16)
            return carry

        lax.fori_loop(0, HALF // 256, tile, 0)

    @staticmethod
    def add(dst, *others):
        def tile(n, carry):
            cols = pl.ds(aligned(n * 256, 256), 256)
            total = dst[:, cols].astype(F32)
            for other in others:
                total = total + other[:, cols].astype(F32)
            dst[:, cols] = total.astype(BF16)
            return carry

        lax.fori_loop(0, HALF // 256, tile, 0)

    def send(self, name, src, slot, p, target, half=None):
        dst = self.got.at[p, slot]
        if half is not None:
            dst = self.got.at[p, slot, pl.ds(half * 32, 32)]
        self.sent.setdefault((name, p), []).append(self.copies.new(src, dst, target))

    def arrived(self, name, p):
        for copy in self.sent[name, p]:
            copy.wait_recv()

    def first(self):
        at = self.at
        g_zp = self.gate(at.zp)
        g_zm = self.gate(at.zm)
        zp_other, zp_own = self.compute(at.zp, 0)
        zm_other, zm_own = self.compute(at.zm, 0)
        g_zz = self.gate(at.zz)
        self.factor(g_zp)
        self.pair(at.zp, at.hh, 0, zp_other)
        self.send("u5", self.mine(at.zp, at.hh, 0), 1, 0, at.up)
        self.factor(g_zm)
        self.pair(at.zm, at.hh, 0, zm_other)
        self.send("d5", self.mine(at.zm, at.hh, 0), 2, 0, at.down)
        zz_other, zz_own = self.compute(at.zz, 0)
        g_z = self.gate(at.z)
        self.factor(g_zz)
        self.pair(at.zz, at.hh, 0, zz_other)
        self.send("y1", self.mine(at.zz, at.hh, 0), 0, 0, at.across)
        self.pair(at.zp, at.h, 0, zp_own)
        self.send("u4", self.mine(at.zp, at.h, 0, 0), 3, 0, at.up, 0)
        self.pair(at.zm, at.h, 0, zm_own)
        self.send("d4", self.mine(at.zm, at.h, 0, 1), 4, 0, at.down, 1)
        self.pair(at.zz, at.h, 0, zz_own)
        z_other, z_own = self.compute(at.z, 0)
        self.factor(g_z)
        self.pair(at.z, at.hh, 0, z_other)
        self.pair(at.z, at.h, 0, z_own)

    def second(self):
        at = self.at
        zp_other, zp_own = self.compute(at.zp, 1)
        zm_other, zm_own = self.compute(at.zm, 1)
        self.pair(at.zp, at.hh, 1, zp_other)
        self.pair(at.zm, at.hh, 1, zm_other)
        self.cross(0)
        self.side(0)
        self.send("u5", self.mine(at.zp, at.hh, 1), 1, 1, at.up)
        self.send("d5", self.mine(at.zm, at.hh, 1), 2, 1, at.down)
        zz_other, zz_own = self.compute(at.zz, 1)
        self.pair(at.zp, at.h, 1, zp_own)
        self.pair(at.zm, at.h, 1, zm_own)
        self.pair(at.zz, at.hh, 1, zz_other)
        self.send("y1", self.mine(at.zz, at.hh, 1), 0, 1, at.across)
        self.join(0)
        self.send("u4", self.mine(at.zp, at.h, 1, 0), 3, 1, at.up, 0)
        self.send("d4", self.mine(at.zm, at.h, 1, 1), 4, 1, at.down, 1)
        self.pair(at.zz, at.h, 1, zz_own)
        z_other, z_own = self.compute(at.z, 1)
        self.pair(at.z, at.hh, 1, z_other)
        self.pair(at.z, at.h, 1, z_own)

    def cross(self, p):
        at = self.at
        self.arrived("y1", p)
        self.add(self.mine(at.zz, at.h, p), self.got.at[p, 0])
        self.send("c_down", self.mine(at.zz, at.h, p, 0), 5, p, at.down, 0)
        self.send("c_up", self.mine(at.zz, at.h, p, 1), 5, p, at.up, 1)

    def side(self, p):
        at = self.at
        self.arrived("u5", p)
        self.arrived("d5", p)
        self.add(self.mine(at.z, at.hh, p), self.got.at[p, 1], self.got.at[p, 2])
        self.send("y6", self.mine(at.z, at.hh, p), 6, p, at.across)

    def join(self, p):
        at = self.at
        self.arrived("c_down", p)
        self.add(self.mine(at.zm, at.h, p, 0), self.got.at[p, 5, pl.ds(0, 32)])
        self.send("d4", self.mine(at.zm, at.h, p, 0), 4, p, at.down, 0)
        self.arrived("c_up", p)
        self.add(self.mine(at.zp, at.h, p, 1), self.got.at[p, 5, pl.ds(32, 32)])
        self.send("u4", self.mine(at.zp, at.h, p, 1), 3, p, at.up, 1)

    def total(self, p, out):
        at = self.at
        for name in ("y6", "u4", "d4"):
            self.arrived(name, p)
        own = self.mine(at.z, at.h, p)

        def tile(n, carry):
            cols = pl.ds(aligned(n * 256, 256), 256)
            wide = pl.ds(aligned(p * HALF + n * 256, 256), 256)
            total = own[:, cols].astype(F32) + self.got[p, 6, :, cols].astype(F32)
            total = total + self.got[p, 3, :, cols].astype(F32) + self.got[p, 4, :, cols].astype(F32)
            out[:, wide] = total.astype(BF16)
            return carry

        lax.fori_loop(0, HALF // 256, tile, 0)


def kernel(
    inflow, fresh, wxz, wproj, wout, conv_w, conv_b, step_b, decay, skip, gain, out,
    act, weight, acc, proj, coded, sums, mixed, states, entering, window, gated, squares,
    part, from_sib, got, stats, scale, received, send_sem, recv_sem, local_sem,
):
    at = Place()
    pair = at.z // 2
    here = pl.ds(aligned(at.me * ROWS, ROWS), ROWS)
    loads = []
    for index, (src, dst) in enumerate(
        [
            (inflow, act.at[here]),
            (wxz, weight.at[:, pl.ds(0, 2 * CHAN)]),
            (wproj.at[:, pl.ds(aligned(pair * 128, 128), 128)], weight.at[:, pl.ds(512, 128)]),
            (wproj.at[:, pl.ds(aligned(256 + pair * 128, 128), 128)], weight.at[:, pl.ds(640, 128)]),
            (wproj.at[:, pl.ds(512, 128)], weight.at[:, pl.ds(768, 128)]),
        ]
    ):
        load = pltpu.make_async_copy(src, dst, local_sem.at[index])
        load.start()
        loads.append(load)
    at.meet()
    copies = Copies(send_sem, recv_sem)
    mixer = Mixer(
        at, (conv_w, conv_b, step_b, decay, skip, gain),
        proj, coded, sums, mixed, states, entering, window, gated, squares,
    )
    scatter_refs = (wout, part, from_sib, got, stats, scale)

    gather = Gather(at, copies, inflow, act, weight, acc, proj)
    gather.own(0)
    gather.own(1)
    gather.near(0)
    for load in loads:
        load.wait()

    @pl.when(at.sec == 0)
    def _():
        load = pltpu.make_async_copy(fresh, received, local_sem.at[0])
        load.start()
        load.wait()

    gather.rest(mixer)
    copies.finish()

    scatter = Scatter(at, copies, mixer, *scatter_refs)
    hops = [copies.make(out.at[0, :, columns(p)], received.at[:, columns(p)], at.after) for p in (0, 1)]

    def relay(p):
        scatter.total(p, out.at[0])
        pl.when(at.sec < LAST)(hops[p].start)

    def relayed(p):
        pl.when(at.sec > 0)(hops[p].wait_recv)
        keep = pltpu.make_async_copy(
            received.at[:, columns(p)], act.at[here, columns(p)], local_sem.at[p]
        )
        keep.start()
        gather.own(p)
        return keep

    scatter.first()
    scatter.second()
    relay(0)
    scatter.cross(1)
    scatter.side(1)
    scatter.join(1)
    gather = Gather(at, copies, received, act, weight, acc, proj)
    keeps = [relayed(0)]
    relay(1)
    gather.near(0)
    keeps.append(relayed(1))
    for keep in keeps:
        keep.wait()
    gather.rest(mixer)
    for p in (0, 1):
        pl.when(at.sec < LAST)(hops[p].wait_send)
    copies.finish()

    scatter = Scatter(at, copies, mixer, *scatter_refs)
    scatter.first()
    scatter.second()
    scatter.cross(1)
    scatter.side(1)
    scatter.total(0, out.at[1])
    scatter.join(1)
    scatter.total(1, out.at[1])
    copies.finish()


def on_device(
    inflow,
    fresh,
    proj_weight,
    xz_weight,
    conv_weight,
    conv_bias,
    step_bias,
    decay_log,
    skip_weight,
    norm_gain,
    out_weight,
):
    anywhere = pl.BlockSpec(memory_space=pl.ANY)
    vmem = pl.BlockSpec(memory_space=pltpu.VMEM)
    out = pl.pallas_call(
        kernel,
        out_shape=jax.ShapeDtypeStruct((2, ROWS, WIDTH), BF16),
        in_specs=[anywhere] * 4 + [vmem] * 7,
        out_specs=vmem,
        scratch_shapes=[
            pltpu.VMEM((TOKENS, WIDTH), BF16),
            pltpu.VMEM((WIDTH, COLS), BF16),
            pltpu.VMEM((TOKENS, COLS), F32),
            pltpu.VMEM((TOKENS + PAD, COLS), BF16),
            pltpu.VMEM((TOKENS, 128), BF16),
            pltpu.VMEM((TOKENS, CHAN), F32),
            pltpu.VMEM((TOKENS, CHAN), F32),
            pltpu.VMEM((TOKENS, CHAN), F32),
            pltpu.VMEM((TOKENS, CHAN), BF16),
            pltpu.VMEM((BLOCK + PAD, 512), F32),
            pltpu.VMEM((TOKENS, CHAN), BF16),
            pltpu.VMEM((8, TOKENS), F32),
            pltpu.VMEM((TOKENS, WIDTH), BF16),
            pltpu.VMEM((TOKENS // 2, WIDTH), BF16),
            pltpu.VMEM((2, LAST, ROWS, HALF), BF16),
            pltpu.VMEM((3, 8, TOKENS), F32),
            pltpu.VMEM((TOKENS, 128), F32),
            pltpu.VMEM((ROWS, WIDTH), BF16),
            pltpu.SemaphoreType.DMA((COPIES,)),
            pltpu.SemaphoreType.DMA((COPIES,)),
            pltpu.SemaphoreType.DMA((5,)),
        ],
        compiler_params=pltpu.CompilerParams(
            collective_id=0, has_side_effects=True, vmem_limit_bytes=60 * MIB
        ),
        name="relay_window",
    )(
        inflow[0], fresh[0], xz_weight[0].reshape(WIDTH, 2 * CHAN), proj_weight[0], out_weight[0],
        conv_weight[0], conv_bias, step_bias, decay_log, skip_weight, norm_gain,
    )
    return out.astype(F32)[None]


def solution(mesh):
    placed = (
        P("section", "seq", None),
        P(None, "seq", None),
        P("section", None, None),
        P("section", None, None, "seq"),
        P("section", None, None),
        P("section", None),
        P("section", None),
        P("section", None),
        P("section", None),
        P("section", None),
        P("section", "seq", None),
    )
    return jax.shard_map(
        on_device,
        mesh=mesh,
        in_specs=placed,
        out_specs=P("section", None, "seq", None),
        check_vma=False,
    )
```

```python
import functools

import jax
import jax.numpy as jnp
from jax import lax
from jax.experimental import pallas as pl
from jax.experimental.pallas import tpu as pltpu
from jax.sharding import PartitionSpec as P

MESH = pl.DeviceIdType.MESH
F32 = jnp.float32
BF16 = jnp.bfloat16
HIGHEST = lax.Precision.HIGHEST
TOKENS = 1024
WIDTH = 4096
CHAN = 256
BLOCK = 128
BLOCKS = TOKENS // BLOCK
ROWS = 64
HALF = WIDTH // 2
COLS = 896
TILES = ((0, 256), (256, 256), (512, 256), (768, 128))
LAST = 7
PAD = 16
COPIES = 192
MIB = 2**20


def aligned(value, by):
    return pl.multiple_of(value, by)


def iota(shape, dim):
    return lax.broadcasted_iota(jnp.int32, shape, dim)


def columns(p):
    return pl.ds(p * HALF, HALF)


class Place:
    def __init__(self):
        self.sec = lax.axis_index("section")
        self.me = lax.axis_index("seq")
        self.z, self.h, self.c = self.me // 4, (self.me // 2) % 2, self.me % 2
        self.zp, self.zm, self.zz = (self.z + 1) % 4, (self.z + 3) % 4, (self.z + 2) % 4
        self.hh = 1 - self.h
        self.up = self.device(self.zp, self.h, self.c)
        self.down = self.device(self.zm, self.h, self.c)
        self.across = self.device(self.z, self.hh, self.c)
        self.sib = self.device(self.z, self.h, 1 - self.c)
        self.diag = self.device(self.z, self.hh, 1 - self.c)
        self.after = ((self.sec + 1) % 8, self.me)
        self.ahead = ((self.sec + 7) % 8, self.me)

    def device(self, z, h, c):
        return (self.sec, z * 4 + h * 2 + c)

    def meet(self):
        targets = [self.up, self.down, self.across, self.sib, self.diag, self.after, self.ahead]
        barrier = pltpu.get_barrier_semaphore()
        for target in targets:
            pl.semaphore_signal(barrier, inc=1, device_id=target, device_id_type=MESH)
        pl.semaphore_wait(barrier, len(targets))


class Copies:
    def __init__(self, send_sem, recv_sem):
        self.send_sem, self.recv_sem = send_sem, recv_sem
        self.count = 0
        self.open = []

    def make(self, src, dst, target):
        index = self.count
        self.count += 1
        return pltpu.make_async_remote_copy(
            src_ref=src,
            dst_ref=dst,
            send_sem=self.send_sem.at[index],
            recv_sem=self.recv_sem.at[index],
            device_id=target,
            device_id_type=MESH,
        )

    def new(self, src, dst, target):
        copy = self.make(src, dst, target)
        copy.start()
        self.open.append(copy)
        return copy

    def finish(self):
        for copy in self.open:
            copy.wait_send()
        self.open = []


class Gather:
    def __init__(self, at, copies, source, act, weight, acc, proj):
        self.at, self.copies, self.source = at, copies, source
        self.act, self.weight, self.acc, self.proj = act, weight, acc, proj
        self.got = {}

    def rows(self, z, h, p, half=None):
        start = (z * 2 + h) * 128 + self.at.c * ROWS
        if half is None:
            return self.act.at[pl.ds(aligned(start, ROWS), ROWS), columns(p)]
        return self.act.at[pl.ds(aligned(start + half * 32, 32), 32), columns(p)]

    def forward(self, z, h, p, target, half=None):
        return self.copies.new(self.rows(z, h, p, half), self.rows(z, h, p, half), target)

    def share(self, name, z, h, p, half=None):
        self.got.setdefault((name, p), []).append(self.forward(z, h, p, self.at.sib, half))

    def own(self, p):
        at = self.at
        src = self.source.at[:, columns(p)]
        dst = self.rows(at.z, at.h, p)
        for name, target in (("up", at.up), ("down", at.down), ("across", at.across), ("own", at.sib)):
            self.got[name, p] = [self.copies.new(src, dst, target)]

    def arrived(self, name, p):
        for copy in self.got[name, p]:
            copy.wait_recv()

    def near(self, p):
        at = self.at
        self.arrived("up", p)
        self.got["cu", p] = [self.forward(at.zm, at.h, p, at.up, 0)]
        self.arrived("down", p)
        self.got["cd", p] = [self.forward(at.zp, at.h, p, at.down, 1)]
        self.share("s_zm", at.zm, at.h, p)
        self.share("s_zp", at.zp, at.h, p)
        self.arrived("across", p)
        self.got["pu", p] = [self.forward(at.z, at.hh, p, at.up)]
        self.got["pd", p] = [self.forward(at.z, at.hh, p, at.down)]
        self.share("s_p", at.z, at.hh, p)

    def far(self, p):
        at = self.at
        for name, half in (("cu", 0), ("cd", 1)):
            self.arrived(name, p)
            self.got["cy%d" % half, p] = [self.forward(at.zz, at.h, p, at.across, half)]
            self.share("s_c", at.zz, at.h, p, half)

    def beside(self, p):
        at = self.at
        self.arrived("pu", p)
        self.share("s_pm", at.zm, at.hh, p)
        self.arrived("pd", p)
        self.share("s_pp", at.zp, at.hh, p)

    def last(self, p):
        at = self.at
        for half in (0, 1):
            self.arrived("cy%d" % half, p)
            self.share("s_cy", at.zz, at.hh, p, half)

    def project(self, name, z, h, p):
        self.arrived(name, p)
        start = (z * 2 + h) * 128
        at = pl.ds(aligned(start, 128), 128)
        padded = pl.ds(aligned(start + PAD, PAD), 128)
        for first, size in TILES:
            cols = pl.ds(first, size)
            part = jnp.dot(
                self.act[at, columns(p)], self.weight[columns(p), cols], preferred_element_type=F32
            )
            if p == 0:
                self.acc[at, cols] = part
            else:
                self.proj[padded, cols] = (self.acc[at, cols] + part).astype(BF16)

    def project_near(self, p):
        at = self.at
        self.project("own", at.z, at.h, p)
        self.project("s_zm", at.zm, at.h, p)
        self.project("s_zp", at.zp, at.h, p)
        self.project("s_p", at.z, at.hh, p)

    def project_beside(self, p):
        at = self.at
        self.project("s_pm", at.zm, at.hh, p)
        self.project("s_pp", at.zp, at.hh, p)

    def rest(self, mixer, separate=None):
        at = self.at
        self.project_near(0)
        self.near(1)
        self.far(0)
        if separate is not None:
            separate(1)
        self.project_near(1)
        self.beside(0)
        self.project("s_c", at.zz, at.h, 0)
        self.far(1)
        mixer.local(0)
        self.project_beside(0)
        self.last(0)
        self.project("s_c", at.zz, at.h, 1)
        self.beside(1)
        self.project("s_cy", at.zz, at.hh, 0)
        self.project_beside(1)
        mixer.local(1)
        self.last(1)
        mixer.local(2)
        self.project("s_cy", at.zz, at.hh, 1)
        mixer.local(3)
        mixer.chain()


class Mixer:
    def __init__(self, at, params, proj, coded, sums, mixed, states, entering, window, gated, squares):
        self.proj, self.coded, self.sums, self.mixed = proj, coded, sums, mixed
        self.states, self.entering, self.window = states, entering, window
        self.gated, self.squares = gated, squares
        conv_w, conv_b, step_b, decay, skip, gain = params
        group = at.me // 4
        x_at = aligned(at.me * CHAN, CHAN)
        b_at = aligned(4096 + (group // 2) * 128, 128)
        c_at = aligned(4352 + (group // 2) * 128, 128)

        def own(ref):
            return jnp.concatenate(
                [ref[:, pl.ds(x_at, CHAN)], ref[:, pl.ds(b_at, 128)], ref[:, pl.ds(c_at, 128)]], axis=1
            )

        spread = (iota((128, CHAN), 0) == at.me * 8 + iota((128, CHAN), 1) // 32).astype(F32)

        def per_channel(ref):
            wide = jnp.broadcast_to(ref[...], (8, 128))
            return jnp.dot(wide, spread, precision=HIGHEST, preferred_element_type=F32)[0:1]

        self.taps, self.offset = own(conv_w), own(conv_b)
        self.bias = per_channel(step_b)
        self.rate = -jnp.exp(per_channel(decay))
        self.direct = per_channel(skip)
        self.gains = gain[:, pl.ds(x_at, CHAN)]
        self.spread = spread.astype(BF16)
        self.half = group % 2
        one, two = at.hh, at.h
        self.order = [
            one * (2 * at.z + 1) + two * (2 * at.z),
            one * (2 * at.zp) + two * (2 * at.z + 1),
            one * (2 * at.z) + two * (2 * at.zp),
            one * (2 * at.zm + 1) + two * (2 * at.zp + 1),
            one * (2 * at.zp + 1) + two * (2 * at.zm),
            one * (2 * at.zz) + two * (2 * at.zm + 1),
            one * (2 * at.zm) + two * (2 * at.zz),
            2 * at.zz + 1,
        ]
        proj[0:PAD, :] = jnp.zeros((PAD, COLS), BF16)

    def local(self, pair):
        first, second = self.order[2 * pair], self.order[2 * pair + 1]
        taps, window = self.taps, self.window
        lower = iota((BLOCK, BLOCK), 0) >= iota((BLOCK, BLOCK), 1)
        lower_ones = lower.astype(F32)
        own_half = iota((BLOCK, 128), 1) // 64 == self.half
        head_of = iota((BLOCK, CHAN), 1) // 32

        def block(index, carry):
            start = ((1 - index) * first + index * second) * BLOCK
            at = pl.ds(aligned(start, BLOCK), BLOCK)
            rows = pl.ds(aligned(start + PAD, PAD), BLOCK)
            window[0:PAD, :] = self.proj[pl.ds(aligned(start, PAD), PAD), pl.ds(256, 512)].astype(F32)
            window[PAD : PAD + BLOCK, :] = self.proj[rows, pl.ds(256, 512)].astype(F32)
            conv = self.offset + taps[0:1] * window[PAD - 3 : PAD - 3 + BLOCK, :]
            for k in range(1, 4):
                conv = conv + taps[k : k + 1] * window[PAD - 3 + k : PAD - 3 + k + BLOCK, :]
            conv = (conv / (1.0 + jnp.exp(-conv))).astype(BF16)
            x = conv[:, :CHAN]
            b = conv[:, CHAN : CHAN + 128]
            c = jnp.where(own_half, conv[:, CHAN + 128 :], jnp.zeros((), BF16))
            self.coded[at, :] = c
            step = jax.nn.softplus(
                jnp.dot(self.proj[rows, pl.ds(768, 128)], self.spread, preferred_element_type=F32)
                + self.bias
            )
            cumulus = jnp.dot(
                lower_ones, self.rate * step, precision=HIGHEST, preferred_element_type=F32
            )
            self.sums[at, :] = cumulus
            cumulus_t = cumulus.T
            step_t = step.T
            scores = lax.dot_general(c, b, (((1,), (1,)), ((), ())), preferred_element_type=F32)
            mixing, values = [], []
            for head in range(8):
                lane = 32 * head
                gap = cumulus[:, lane : lane + 1] - cumulus_t[lane : lane + 1, :]
                gap = jnp.where(lower, gap, -1e30)
                mixing.append((scores * jnp.exp(gap) * step_t[lane : lane + 1, :]).astype(BF16))
                values.append(jnp.where(head_of == head, x, jnp.zeros((), BF16)))
            diagonal = jnp.dot(
                jnp.concatenate(mixing, axis=1),
                jnp.concatenate(values, axis=0),
                preferred_element_type=F32,
            )
            x32 = x.astype(F32)
            self.mixed[at, :] = diagonal + self.direct * x32
            total = cumulus[BLOCK - 1 : BLOCK]
            weighted = (x32 * (jnp.exp(total - cumulus) * step)).astype(BF16)
            self.states[at, :] = lax.dot_general(
                b, weighted, (((0,), (0,)), ((), ())), preferred_element_type=F32
            )
            return carry

        lax.fori_loop(0, 2, block, 0)

    def chain(self):
        state = jnp.zeros((BLOCK, CHAN), F32)
        for index in range(BLOCKS):
            at = pl.ds(index * BLOCK, BLOCK)
            self.entering[at, :] = state.astype(BF16)
            if index < BLOCKS - 1:
                total = self.sums[(index + 1) * BLOCK - 1 : (index + 1) * BLOCK, :]
                state = jnp.exp(total) * state + self.states[at, :]

    def outputs(self, z):
        def block(index, carry):
            start = z * 256 + index * BLOCK
            at = pl.ds(aligned(start, BLOCK), BLOCK)
            mixed = self.mixed[at, :] + jnp.exp(self.sums[at, :]) * jnp.dot(
                self.coded[at, :], self.entering[at, :], preferred_element_type=F32
            )
            gate = self.proj[pl.ds(aligned(start + PAD, PAD), BLOCK), pl.ds(0, CHAN)].astype(F32)
            gated = mixed * (gate / (1.0 + jnp.exp(-gate)))
            self.squares[:, at] = lax.dot_general(
                jnp.ones((8, CHAN), F32),
                gated * gated,
                (((1,), (1,)), ((), ())),
                precision=HIGHEST,
                preferred_element_type=F32,
            )
            self.gated[at, :] = (gated * self.gains).astype(BF16)
            return carry

        lax.fori_loop(0, 2, block, 0)


class Scatter:
    def __init__(self, at, copies, mixer, wout, part, from_sib, got, stats, scale):
        self.at, self.copies, self.mixer, self.wout = at, copies, mixer, wout
        self.part, self.from_sib, self.got, self.stats, self.scale = part, from_sib, got, stats, scale
        self.sent = {}

    def gate(self, z):
        self.mixer.outputs(z)
        cols = pl.ds(aligned(z * 256, 256), 256)
        squares = self.mixer.squares.at[:, cols]
        self.shares = [
            self.copies.new(squares, self.stats.at[i, :, cols], target)
            for i, target in enumerate((self.at.sib, self.at.across, self.at.diag))
        ]
        return z, self.shares

    def factor(self, gate):
        z, shares = gate
        for share in shares:
            share.wait_recv()
        for i in (0, 1):
            at = pl.ds(aligned(z * 256 + i * 128, 128), 128)
            total = self.mixer.squares[:, at] + self.stats[0, :, at]
            total = total + self.stats[1, :, at] + self.stats[2, :, at]
            self.scale[at, :] = lax.dot_general(
                lax.rsqrt(total / 1024.0 + 1e-05),
                jnp.full((8, 128), 0.125, F32),
                (((0,), (0,)), ((), ())),
                precision=HIGHEST,
                preferred_element_type=F32,
            )

    def mine(self, z, h, p, half=None):
        start = (z * 2 + h) * 128 + self.at.c * ROWS
        if half is None:
            return self.part.at[pl.ds(aligned(start, ROWS), ROWS), columns(p)]
        return self.part.at[pl.ds(aligned(start + half * 32, 32), 32), columns(p)]

    def compute(self, z, p):
        at = pl.ds(aligned(z * 256, 256), 256)
        lhs = self.mixer.gated[at, :]

        def tile(n, carry):
            cols = pl.ds(aligned(p * HALF + n * 512, 512), 512)
            self.part[at, cols] = jnp.dot(
                lhs, self.wout[:, cols], preferred_element_type=F32
            ).astype(BF16)
            return carry

        lax.fori_loop(0, HALF // 512, tile, 0)
        copies = []
        for h in (self.at.hh, self.at.h):
            start = (z * 2 + h) * 128 + (1 - self.at.c) * ROWS
            src = self.part.at[pl.ds(aligned(start, ROWS), ROWS), columns(p)]
            dst = self.from_sib.at[pl.ds(aligned((z * 2 + h) * ROWS, ROWS), ROWS), columns(p)]
            copies.append(self.copies.new(src, dst, self.at.sib))
        return copies

    def pair(self, z, h, p, copy):
        copy.wait_recv()
        own = self.mine(z, h, p)
        other = self.from_sib.at[pl.ds(aligned((z * 2 + h) * ROWS, ROWS), ROWS), columns(p)]
        rows = pl.ds(aligned((z * 2 + h) * 128 + self.at.c * ROWS, ROWS), ROWS)
        scale = jnp.concatenate([self.scale[rows, :]] * 2, axis=1)

        def tile(n, carry):
            cols = pl.ds(aligned(n * 256, 256), 256)
            total = own[:, cols].astype(F32) + other[:, cols].astype(F32)
            own[:, cols] = (total * scale).astype(BF16)
            return carry

        lax.fori_loop(0, HALF // 256, tile, 0)

    @staticmethod
    def add(dst, *others):
        def tile(n, carry):
            cols = pl.ds(aligned(n * 256, 256), 256)
            total = dst[:, cols].astype(F32)
            for other in others:
                total = total + other[:, cols].astype(F32)
            dst[:, cols] = total.astype(BF16)
            return carry

        lax.fori_loop(0, HALF // 256, tile, 0)

    def send(self, name, src, slot, p, target, half=None):
        dst = self.got.at[p, slot]
        if half is not None:
            dst = self.got.at[p, slot, pl.ds(half * 32, 32)]
        self.sent.setdefault((name, p), []).append(self.copies.new(src, dst, target))

    def arrived(self, name, p):
        for copy in self.sent[name, p]:
            copy.wait_recv()

    def first(self):
        at = self.at
        g_zp = self.gate(at.zp)
        g_zm = self.gate(at.zm)
        zp_other, zp_own = self.compute(at.zp, 0)
        zm_other, zm_own = self.compute(at.zm, 0)
        g_zz = self.gate(at.zz)
        self.factor(g_zp)
        self.pair(at.zp, at.hh, 0, zp_other)
        self.send("u5", self.mine(at.zp, at.hh, 0), 1, 0, at.up)
        self.factor(g_zm)
        self.pair(at.zm, at.hh, 0, zm_other)
        self.send("d5", self.mine(at.zm, at.hh, 0), 2, 0, at.down)
        zz_other, zz_own = self.compute(at.zz, 0)
        g_z = self.gate(at.z)
        self.factor(g_zz)
        self.pair(at.zz, at.hh, 0, zz_other)
        self.send("y1", self.mine(at.zz, at.hh, 0), 0, 0, at.across)
        self.pair(at.zp, at.h, 0, zp_own)
        self.send("u4", self.mine(at.zp, at.h, 0, 0), 3, 0, at.up, 0)
        self.pair(at.zm, at.h, 0, zm_own)
        self.send("d4", self.mine(at.zm, at.h, 0, 1), 4, 0, at.down, 1)
        self.pair(at.zz, at.h, 0, zz_own)
        z_other, z_own = self.compute(at.z, 0)
        self.factor(g_z)
        self.pair(at.z, at.hh, 0, z_other)
        self.pair(at.z, at.h, 0, z_own)

    def second(self):
        at = self.at
        zp_other, zp_own = self.compute(at.zp, 1)
        zm_other, zm_own = self.compute(at.zm, 1)
        self.pair(at.zp, at.hh, 1, zp_other)
        self.pair(at.zm, at.hh, 1, zm_other)
        self.cross(0)
        self.side(0)
        self.send("u5", self.mine(at.zp, at.hh, 1), 1, 1, at.up)
        self.send("d5", self.mine(at.zm, at.hh, 1), 2, 1, at.down)
        zz_other, zz_own = self.compute(at.zz, 1)
        self.pair(at.zp, at.h, 1, zp_own)
        self.pair(at.zm, at.h, 1, zm_own)
        self.pair(at.zz, at.hh, 1, zz_other)
        self.send("y1", self.mine(at.zz, at.hh, 1), 0, 1, at.across)
        self.join(0)
        self.send("u4", self.mine(at.zp, at.h, 1, 0), 3, 1, at.up, 0)
        self.send("d4", self.mine(at.zm, at.h, 1, 1), 4, 1, at.down, 1)
        self.pair(at.zz, at.h, 1, zz_own)
        z_other, z_own = self.compute(at.z, 1)
        self.pair(at.z, at.hh, 1, z_other)
        self.pair(at.z, at.h, 1, z_own)

    def cross(self, p):
        at = self.at
        self.arrived("y1", p)
        self.add(self.mine(at.zz, at.h, p), self.got.at[p, 0])
        self.send("c_down", self.mine(at.zz, at.h, p, 0), 5, p, at.down, 0)
        self.send("c_up", self.mine(at.zz, at.h, p, 1), 5, p, at.up, 1)

    def side(self, p):
        at = self.at
        self.arrived("u5", p)
        self.arrived("d5", p)
        self.add(self.mine(at.z, at.hh, p), self.got.at[p, 1], self.got.at[p, 2])
        self.send("y6", self.mine(at.z, at.hh, p), 6, p, at.across)

    def join(self, p):
        at = self.at
        self.arrived("c_down", p)
        self.add(self.mine(at.zm, at.h, p, 0), self.got.at[p, 5, pl.ds(0, 32)])
        self.send("d4", self.mine(at.zm, at.h, p, 0), 4, p, at.down, 0)
        self.arrived("c_up", p)
        self.add(self.mine(at.zp, at.h, p, 1), self.got.at[p, 5, pl.ds(32, 32)])
        self.send("u4", self.mine(at.zp, at.h, p, 1), 3, p, at.up, 1)

    def total(self, p, out):
        at = self.at
        for name in ("y6", "u4", "d4"):
            self.arrived(name, p)
        own = self.mine(at.z, at.h, p)

        def tile(n, carry):
            cols = pl.ds(aligned(n * 256, 256), 256)
            wide = pl.ds(aligned(p * HALF + n * 256, 256), 256)
            total = own[:, cols].astype(F32) + self.got[p, 6, :, cols].astype(F32)
            total = total + self.got[p, 3, :, cols].astype(F32) + self.got[p, 4, :, cols].astype(F32)
            out[:, wide] = total.astype(BF16)
            return carry

        lax.fori_loop(0, HALF // 256, tile, 0)


def kernel(
    inflow, fresh, wxz, wproj, wout, conv_w, conv_b, step_b, decay, skip, gain, out,
    act, raw, weight, acc, proj, coded, sums, mixed, states, entering, window, gated, squares,
    part, from_sib, got, stats, scale, received, send_sem, recv_sem, local_sem,
):
    at = Place()
    pair = at.z // 2
    here = pl.ds(aligned(at.me * ROWS, ROWS), ROWS)
    loads = []
    for index, (src, dst) in enumerate(
        [
            (inflow, act.at[here]),
            (wxz.at[pl.ds(0, HALF)], raw.at[pl.ds(0, HALF)]),
            (wxz.at[pl.ds(HALF, HALF)], raw.at[pl.ds(HALF, HALF)]),
            (wproj.at[:, pl.ds(aligned(pair * 128, 128), 128)], weight.at[:, pl.ds(512, 128)]),
            (wproj.at[:, pl.ds(aligned(256 + pair * 128, 128), 128)], weight.at[:, pl.ds(640, 128)]),
            (wproj.at[:, pl.ds(512, 128)], weight.at[:, pl.ds(768, 128)]),
        ]
    ):
        load = pltpu.make_async_copy(src, dst, local_sem.at[index])
        load.start()
        loads.append(load)
    at.meet()
    copies = Copies(send_sem, recv_sem)
    mixer = Mixer(
        at, (conv_w, conv_b, step_b, decay, skip, gain),
        proj, coded, sums, mixed, states, entering, window, gated, squares,
    )
    scatter_refs = (wout, part, from_sib, got, stats, scale)

    gather = Gather(at, copies, inflow, act, weight, acc, proj)
    gather.own(0)
    gather.own(1)

    def separate(p):
        loads[1 + p].wait()

        def tile(n, carry):
            at = pl.ds(aligned(p * HALF + n * 128, 128), 128)
            weight[at, pl.ds(0, CHAN)] = raw[at, 0, :]
            weight[at, pl.ds(CHAN, CHAN)] = raw[at, 1, :]
            return carry

        lax.fori_loop(0, HALF // 128, tile, 0)

    separate(0)
    gather.near(0)
    for index in (0, 3, 4, 5):
        loads[index].wait()

    @pl.when(at.sec == 0)
    def _():
        load = pltpu.make_async_copy(fresh, received, local_sem.at[0])
        load.start()
        load.wait()

    gather.rest(mixer, separate)
    copies.finish()

    scatter = Scatter(at, copies, mixer, *scatter_refs)
    hops = [copies.make(out.at[0, :, columns(p)], received.at[:, columns(p)], at.after) for p in (0, 1)]

    def relay(p):
        scatter.total(p, out.at[0])
        pl.when(at.sec < LAST)(hops[p].start)

    def relayed(p):
        pl.when(at.sec > 0)(hops[p].wait_recv)
        keep = pltpu.make_async_copy(
            received.at[:, columns(p)], act.at[here, columns(p)], local_sem.at[p]
        )
        keep.start()
        gather.own(p)
        return keep

    scatter.first()
    scatter.second()
    relay(0)
    scatter.cross(1)
    scatter.side(1)
    scatter.join(1)
    gather = Gather(at, copies, received, act, weight, acc, proj)
    keeps = [relayed(0)]
    relay(1)
    gather.near(0)
    keeps.append(relayed(1))
    for keep in keeps:
        keep.wait()
    gather.rest(mixer)
    for p in (0, 1):
        pl.when(at.sec < LAST)(hops[p].wait_send)
    copies.finish()

    scatter = Scatter(at, copies, mixer, *scatter_refs)
    scatter.first()
    scatter.second()
    scatter.cross(1)
    scatter.side(1)
    scatter.total(0, out.at[1])
    scatter.join(1)
    scatter.total(1, out.at[1])
    copies.finish()


def on_device(
    inflow,
    fresh,
    proj_weight,
    xz_weight,
    conv_weight,
    conv_bias,
    step_bias,
    decay_log,
    skip_weight,
    norm_gain,
    out_weight,
):
    anywhere = pl.BlockSpec(memory_space=pl.ANY)
    vmem = pl.BlockSpec(memory_space=pltpu.VMEM)
    out = pl.pallas_call(
        kernel,
        out_shape=jax.ShapeDtypeStruct((2, ROWS, WIDTH), BF16),
        in_specs=[anywhere] * 4 + [vmem] * 7,
        out_specs=vmem,
        scratch_shapes=[
            pltpu.VMEM((TOKENS, WIDTH), BF16),
            pltpu.VMEM((WIDTH, 2, CHAN), BF16),
            pltpu.VMEM((WIDTH, COLS), BF16),
            pltpu.VMEM((TOKENS, COLS), F32),
            pltpu.VMEM((TOKENS + PAD, COLS), BF16),
            pltpu.VMEM((TOKENS, 128), BF16),
            pltpu.VMEM((TOKENS, CHAN), F32),
            pltpu.VMEM((TOKENS, CHAN), F32),
            pltpu.VMEM((TOKENS, CHAN), F32),
            pltpu.VMEM((TOKENS, CHAN), BF16),
            pltpu.VMEM((BLOCK + PAD, 512), F32),
            pltpu.VMEM((TOKENS, CHAN), BF16),
            pltpu.VMEM((8, TOKENS), F32),
            pltpu.VMEM((TOKENS, WIDTH), BF16),
            pltpu.VMEM((TOKENS // 2, WIDTH), BF16),
            pltpu.VMEM((2, LAST, ROWS, HALF), BF16),
            pltpu.VMEM((3, 8, TOKENS), F32),
            pltpu.VMEM((TOKENS, 128), F32),
            pltpu.VMEM((ROWS, WIDTH), BF16),
            pltpu.SemaphoreType.DMA((COPIES,)),
            pltpu.SemaphoreType.DMA((COPIES,)),
            pltpu.SemaphoreType.DMA((6,)),
        ],
        compiler_params=pltpu.CompilerParams(
            collective_id=0, has_side_effects=True, vmem_limit_bytes=60 * MIB
        ),
        name="relay_window",
    )(
        inflow[0], fresh[0], xz_weight[0], proj_weight[0], out_weight[0],
        conv_weight[0], conv_bias, step_bias, decay_log, skip_weight, norm_gain,
    )
    return out.astype(F32)[None]


def solution(mesh):
    placed = (
        P("section", "seq", None),
        P(None, "seq", None),
        P("section", None, None),
        P("section", None, None, "seq"),
        P("section", None, None),
        P("section", None),
        P("section", None),
        P("section", None),
        P("section", None),
        P("section", None),
        P("section", "seq", None),
    )
    return jax.shard_map(
        on_device,
        mesh=mesh,
        in_specs=placed,
        out_specs=P("section", None, "seq", None),
        check_vma=False,
    )
```

```python
import functools

import jax
import jax.numpy as jnp
from jax import lax
from jax.experimental import pallas as pl
from jax.experimental.pallas import tpu as pltpu
from jax.sharding import PartitionSpec as P

MESH = pl.DeviceIdType.MESH
F32 = jnp.float32
BF16 = jnp.bfloat16
HIGHEST = lax.Precision.HIGHEST
TOKENS = 1024
WIDTH = 4096
CHAN = 256
BLOCK = 128
BLOCKS = TOKENS // BLOCK
ROWS = 64
HALF = WIDTH // 2
COLS = 896
TILES = ((0, 256), (256, 256), (512, 256), (768, 128))
LAST = 7
PAD = 16
COPIES = 192
MIB = 2**20


def aligned(value, by):
    return pl.multiple_of(value, by)


def iota(shape, dim):
    return lax.broadcasted_iota(jnp.int32, shape, dim)


def columns(p):
    return pl.ds(p * HALF, HALF)


def parts_of(value, count):
    parts = []
    for _ in range(count):
        part = value.astype(BF16)
        parts.append(part)
        value = value - part.astype(F32)
    return parts


class Place:
    def __init__(self):
        self.sec = lax.axis_index("section")
        self.me = lax.axis_index("seq")
        self.z, self.h, self.c = self.me // 4, (self.me // 2) % 2, self.me % 2
        self.zp, self.zm, self.zz = (self.z + 1) % 4, (self.z + 3) % 4, (self.z + 2) % 4
        self.hh = 1 - self.h
        self.up = self.device(self.zp, self.h, self.c)
        self.down = self.device(self.zm, self.h, self.c)
        self.across = self.device(self.z, self.hh, self.c)
        self.sib = self.device(self.z, self.h, 1 - self.c)
        self.diag = self.device(self.z, self.hh, 1 - self.c)
        self.after = ((self.sec + 1) % 8, self.me)
        self.ahead = ((self.sec + 7) % 8, self.me)

    def device(self, z, h, c):
        return (self.sec, z * 4 + h * 2 + c)

    def meet(self):
        targets = [self.up, self.down, self.across, self.sib, self.diag, self.after, self.ahead]
        barrier = pltpu.get_barrier_semaphore()
        for target in targets:
            pl.semaphore_signal(barrier, inc=1, device_id=target, device_id_type=MESH)
        pl.semaphore_wait(barrier, len(targets))


class Copies:
    def __init__(self, send_sem, recv_sem):
        self.send_sem, self.recv_sem = send_sem, recv_sem
        self.count = 0
        self.open = []

    def make(self, src, dst, target):
        index = self.count
        self.count += 1
        return pltpu.make_async_remote_copy(
            src_ref=src,
            dst_ref=dst,
            send_sem=self.send_sem.at[index],
            recv_sem=self.recv_sem.at[index],
            device_id=target,
            device_id_type=MESH,
        )

    def new(self, src, dst, target):
        copy = self.make(src, dst, target)
        copy.start()
        self.open.append(copy)
        return copy

    def finish(self):
        for copy in self.open:
            copy.wait_send()
        self.open = []


class Gather:
    def __init__(self, at, copies, source, act, weight, acc, proj):
        self.at, self.copies, self.source = at, copies, source
        self.act, self.weight, self.acc, self.proj = act, weight, acc, proj
        self.got = {}

    def rows(self, z, h, p, half=None):
        start = (z * 2 + h) * 128 + self.at.c * ROWS
        if half is None:
            return self.act.at[pl.ds(aligned(start, ROWS), ROWS), columns(p)]
        return self.act.at[pl.ds(aligned(start + half * 32, 32), 32), columns(p)]

    def forward(self, z, h, p, target, half=None):
        return self.copies.new(self.rows(z, h, p, half), self.rows(z, h, p, half), target)

    def share(self, name, z, h, p, half=None):
        self.got.setdefault((name, p), []).append(self.forward(z, h, p, self.at.sib, half))

    def own(self, p):
        at = self.at
        src = self.source.at[:, columns(p)]
        dst = self.rows(at.z, at.h, p)
        for name, target in (("up", at.up), ("down", at.down), ("across", at.across), ("own", at.sib)):
            self.got[name, p] = [self.copies.new(src, dst, target)]

    def arrived(self, name, p):
        for copy in self.got[name, p]:
            copy.wait_recv()

    def near(self, p):
        at = self.at
        self.arrived("up", p)
        self.got["cu", p] = [self.forward(at.zm, at.h, p, at.up, 0)]
        self.arrived("down", p)
        self.got["cd", p] = [self.forward(at.zp, at.h, p, at.down, 1)]
        self.share("s_zm", at.zm, at.h, p)
        self.share("s_zp", at.zp, at.h, p)
        self.arrived("across", p)
        self.got["pu", p] = [self.forward(at.z, at.hh, p, at.up)]
        self.got["pd", p] = [self.forward(at.z, at.hh, p, at.down)]
        self.share("s_p", at.z, at.hh, p)

    def far(self, p):
        at = self.at
        for name, half in (("cu", 0), ("cd", 1)):
            self.arrived(name, p)
            self.got["cy%d" % half, p] = [self.forward(at.zz, at.h, p, at.across, half)]
            self.share("s_c", at.zz, at.h, p, half)

    def beside(self, p):
        at = self.at
        self.arrived("pu", p)
        self.share("s_pm", at.zm, at.hh, p)
        self.arrived("pd", p)
        self.share("s_pp", at.zp, at.hh, p)

    def last(self, p):
        at = self.at
        for half in (0, 1):
            self.arrived("cy%d" % half, p)
            self.share("s_cy", at.zz, at.hh, p, half)

    def project(self, name, z, h, p):
        self.arrived(name, p)
        start = (z * 2 + h) * 128
        at = pl.ds(aligned(start, 128), 128)
        padded = pl.ds(aligned(start + PAD, PAD), 128)
        for first, size in TILES:
            cols = pl.ds(first, size)
            part = jnp.dot(
                self.act[at, columns(p)], self.weight[columns(p), cols], preferred_element_type=F32
            )
            if p == 0:
                self.acc[at, cols] = part
            else:
                self.proj[padded, cols] = (self.acc[at, cols] + part).astype(BF16)

    def project_near(self, p):
        at = self.at
        self.project("own", at.z, at.h, p)
        self.project("s_zm", at.zm, at.h, p)
        self.project("s_zp", at.zp, at.h, p)
        self.project("s_p", at.z, at.hh, p)

    def project_beside(self, p):
        at = self.at
        self.project("s_pm", at.zm, at.hh, p)
        self.project("s_pp", at.zp, at.hh, p)

    def rest(self, mixer, separate=None):
        at = self.at
        self.project_near(0)
        self.near(1)
        self.far(0)
        if separate is not None:
            separate(1)
        self.project_near(1)
        self.beside(0)
        self.project("s_c", at.zz, at.h, 0)
        self.far(1)
        mixer.local(0)
        self.project_beside(0)
        self.last(0)
        self.project("s_c", at.zz, at.h, 1)
        self.beside(1)
        self.project("s_cy", at.zz, at.hh, 0)
        self.project_beside(1)
        mixer.local(1)
        self.last(1)
        mixer.local(2)
        self.project("s_cy", at.zz, at.hh, 1)
        mixer.local(3)
        mixer.chain()


class Mixer:
    def __init__(self, at, params, proj, coded, sums, mixed, states, entering, window, gated, squares):
        self.proj, self.coded, self.sums, self.mixed = proj, coded, sums, mixed
        self.states, self.entering, self.window = states, entering, window
        self.gated, self.squares = gated, squares
        conv_w, conv_b, step_b, decay, skip, gain = params
        group = at.me // 4
        x_at = aligned(at.me * CHAN, CHAN)
        b_at = aligned(4096 + (group // 2) * 128, 128)
        c_at = aligned(4352 + (group // 2) * 128, 128)

        def own(ref):
            return jnp.concatenate(
                [ref[:, pl.ds(x_at, CHAN)], ref[:, pl.ds(b_at, 128)], ref[:, pl.ds(c_at, 128)]], axis=1
            )

        spread = (iota((128, CHAN), 0) == at.me * 8 + iota((128, CHAN), 1) // 32).astype(F32)

        def per_channel(ref):
            wide = jnp.broadcast_to(ref[...], (8, 128))
            return jnp.dot(wide, spread, precision=HIGHEST, preferred_element_type=F32)[0:1]

        self.taps, self.offset = own(conv_w), own(conv_b)
        self.bias = per_channel(step_b)
        self.rate = -jnp.exp(per_channel(decay))
        self.direct = per_channel(skip)
        self.gains = gain[:, pl.ds(x_at, CHAN)]
        self.spread = spread.astype(BF16)
        self.half = group % 2
        one, two = at.hh, at.h
        self.order = [
            one * (2 * at.z + 1) + two * (2 * at.z),
            one * (2 * at.zp) + two * (2 * at.z + 1),
            one * (2 * at.z) + two * (2 * at.zp),
            one * (2 * at.zm + 1) + two * (2 * at.zp + 1),
            one * (2 * at.zp + 1) + two * (2 * at.zm),
            one * (2 * at.zz) + two * (2 * at.zm + 1),
            one * (2 * at.zm) + two * (2 * at.zz),
            2 * at.zz + 1,
        ]
        proj[0:PAD, :] = jnp.zeros((PAD, COLS), BF16)

    def local(self, pair):
        first, second = self.order[2 * pair], self.order[2 * pair + 1]
        taps, window = self.taps, self.window
        lower = iota((BLOCK, BLOCK), 0) >= iota((BLOCK, BLOCK), 1)
        lower_ones = lower.astype(F32).astype(BF16)
        own_half = iota((BLOCK, 128), 1) // 64 == self.half
        head_of = iota((BLOCK, CHAN), 1) // 32

        def block(index, carry):
            start = ((1 - index) * first + index * second) * BLOCK
            at = pl.ds(aligned(start, BLOCK), BLOCK)
            rows = pl.ds(aligned(start + PAD, PAD), BLOCK)
            window[0:PAD, :] = self.proj[pl.ds(aligned(start, PAD), PAD), pl.ds(256, 512)].astype(F32)
            window[PAD : PAD + BLOCK, :] = self.proj[rows, pl.ds(256, 512)].astype(F32)
            conv = self.offset + taps[0:1] * window[PAD - 3 : PAD - 3 + BLOCK, :]
            for k in range(1, 4):
                conv = conv + taps[k : k + 1] * window[PAD - 3 + k : PAD - 3 + k + BLOCK, :]
            conv = (conv / (1.0 + jnp.exp(-conv))).astype(BF16)
            x = conv[:, :CHAN]
            b = conv[:, CHAN : CHAN + 128]
            c = jnp.where(own_half, conv[:, CHAN + 128 :], jnp.zeros((), BF16))
            self.coded[at, :] = c
            step = jax.nn.softplus(
                jnp.dot(self.proj[rows, pl.ds(768, 128)], self.spread, preferred_element_type=F32)
                + self.bias
            )
            cumulus = jnp.zeros((BLOCK, CHAN), F32)
            for part in parts_of(self.rate * step, 3):
                cumulus = cumulus + jnp.dot(lower_ones, part, preferred_element_type=F32)
            self.sums[at, :] = cumulus
            cumulus_t = cumulus.T
            step_t = step.T
            scores = lax.dot_general(c, b, (((1,), (1,)), ((), ())), preferred_element_type=F32)
            mixing, values = [], []
            for head in range(8):
                lane = 32 * head
                gap = cumulus[:, lane : lane + 1] - cumulus_t[lane : lane + 1, :]
                gap = jnp.where(lower, gap, -1e30)
                mixing.append((scores * jnp.exp(gap) * step_t[lane : lane + 1, :]).astype(BF16))
                values.append(jnp.where(head_of == head, x, jnp.zeros((), BF16)))
            diagonal = jnp.dot(
                jnp.concatenate(mixing, axis=1),
                jnp.concatenate(values, axis=0),
                preferred_element_type=F32,
            )
            x32 = x.astype(F32)
            self.mixed[at, :] = diagonal + self.direct * x32
            total = cumulus[BLOCK - 1 : BLOCK]
            weighted = (x32 * (jnp.exp(total - cumulus) * step)).astype(BF16)
            self.states[at, :] = lax.dot_general(
                b, weighted, (((0,), (0,)), ((), ())), preferred_element_type=F32
            )
            return carry

        lax.fori_loop(0, 2, block, 0)

    def chain(self):
        state = jnp.zeros((BLOCK, CHAN), F32)
        for index in range(BLOCKS):
            at = pl.ds(index * BLOCK, BLOCK)
            self.entering[at, :] = state.astype(BF16)
            if index < BLOCKS - 1:
                total = self.sums[(index + 1) * BLOCK - 1 : (index + 1) * BLOCK, :]
                state = jnp.exp(total) * state + self.states[at, :]

    def outputs(self, z):
        def block(index, carry):
            start = z * 256 + index * BLOCK
            at = pl.ds(aligned(start, BLOCK), BLOCK)
            mixed = self.mixed[at, :] + jnp.exp(self.sums[at, :]) * jnp.dot(
                self.coded[at, :], self.entering[at, :], preferred_element_type=F32
            )
            gate = self.proj[pl.ds(aligned(start + PAD, PAD), BLOCK), pl.ds(0, CHAN)].astype(F32)
            gated = mixed * (gate / (1.0 + jnp.exp(-gate)))
            total = jnp.zeros((8, BLOCK), F32)
            for part in parts_of(gated * gated, 2):
                total = total + lax.dot_general(
                    jnp.ones((8, CHAN), BF16), part, (((1,), (1,)), ((), ())), preferred_element_type=F32
                )
            self.squares[:, at] = total
            self.gated[at, :] = (gated * self.gains).astype(BF16)
            return carry

        lax.fori_loop(0, 2, block, 0)


class Scatter:
    def __init__(self, at, copies, mixer, wout, part, from_sib, got, stats, scale):
        self.at, self.copies, self.mixer, self.wout = at, copies, mixer, wout
        self.part, self.from_sib, self.got, self.stats, self.scale = part, from_sib, got, stats, scale
        self.sent = {}

    def gate(self, z):
        self.mixer.outputs(z)
        cols = pl.ds(aligned(z * 256, 256), 256)
        squares = self.mixer.squares.at[:, cols]
        self.shares = [
            self.copies.new(squares, self.stats.at[i, :, cols], target)
            for i, target in enumerate((self.at.sib, self.at.across, self.at.diag))
        ]
        return z, self.shares

    def factor(self, gate):
        z, shares = gate
        for share in shares:
            share.wait_recv()
        for i in (0, 1):
            at = pl.ds(aligned(z * 256 + i * 128, 128), 128)
            total = self.mixer.squares[:, at] + self.stats[0, :, at]
            total = total + self.stats[1, :, at] + self.stats[2, :, at]
            self.scale[at, :] = lax.dot_general(
                lax.rsqrt(total / 1024.0 + 1e-05),
                jnp.full((8, 128), 0.125, F32),
                (((0,), (0,)), ((), ())),
                precision=HIGHEST,
                preferred_element_type=F32,
            )

    def mine(self, z, h, p, half=None):
        start = (z * 2 + h) * 128 + self.at.c * ROWS
        if half is None:
            return self.part.at[pl.ds(aligned(start, ROWS), ROWS), columns(p)]
        return self.part.at[pl.ds(aligned(start + half * 32, 32), 32), columns(p)]

    def compute(self, z, p):
        at = pl.ds(aligned(z * 256, 256), 256)
        lhs = self.mixer.gated[at, :]

        def tile(n, carry):
            cols = pl.ds(aligned(p * HALF + n * 512, 512), 512)
            self.part[at, cols] = jnp.dot(
                lhs, self.wout[:, cols], preferred_element_type=F32
            ).astype(BF16)
            return carry

        lax.fori_loop(0, HALF // 512, tile, 0)
        copies = []
        for h in (self.at.hh, self.at.h):
            start = (z * 2 + h) * 128 + (1 - self.at.c) * ROWS
            src = self.part.at[pl.ds(aligned(start, ROWS), ROWS), columns(p)]
            dst = self.from_sib.at[pl.ds(aligned((z * 2 + h) * ROWS, ROWS), ROWS), columns(p)]
            copies.append(self.copies.new(src, dst, self.at.sib))
        return copies

    def pair(self, z, h, p, copy):
        copy.wait_recv()
        own = self.mine(z, h, p)
        other = self.from_sib.at[pl.ds(aligned((z * 2 + h) * ROWS, ROWS), ROWS), columns(p)]
        rows = pl.ds(aligned((z * 2 + h) * 128 + self.at.c * ROWS, ROWS), ROWS)
        scale = jnp.concatenate([self.scale[rows, :]] * 2, axis=1)

        def tile(n, carry):
            cols = pl.ds(aligned(n * 256, 256), 256)
            total = own[:, cols].astype(F32) + other[:, cols].astype(F32)
            own[:, cols] = (total * scale).astype(BF16)
            return carry

        lax.fori_loop(0, HALF // 256, tile, 0)

    @staticmethod
    def add(dst, *others):
        def tile(n, carry):
            cols = pl.ds(aligned(n * 256, 256), 256)
            total = dst[:, cols].astype(F32)
            for other in others:
                total = total + other[:, cols].astype(F32)
            dst[:, cols] = total.astype(BF16)
            return carry

        lax.fori_loop(0, HALF // 256, tile, 0)

    def send(self, name, src, slot, p, target, half=None):
        dst = self.got.at[p, slot]
        if half is not None:
            dst = self.got.at[p, slot, pl.ds(half * 32, 32)]
        self.sent.setdefault((name, p), []).append(self.copies.new(src, dst, target))

    def arrived(self, name, p):
        for copy in self.sent[name, p]:
            copy.wait_recv()

    def first(self):
        at = self.at
        g_zp = self.gate(at.zp)
        g_zm = self.gate(at.zm)
        zp_other, zp_own = self.compute(at.zp, 0)
        zm_other, zm_own = self.compute(at.zm, 0)
        g_zz = self.gate(at.zz)
        self.factor(g_zp)
        self.pair(at.zp, at.hh, 0, zp_other)
        self.send("u5", self.mine(at.zp, at.hh, 0), 1, 0, at.up)
        self.factor(g_zm)
        self.pair(at.zm, at.hh, 0, zm_other)
        self.send("d5", self.mine(at.zm, at.hh, 0), 2, 0, at.down)
        zz_other, zz_own = self.compute(at.zz, 0)
        g_z = self.gate(at.z)
        self.factor(g_zz)
        self.pair(at.zz, at.hh, 0, zz_other)
        self.send("y1", self.mine(at.zz, at.hh, 0), 0, 0, at.across)
        self.pair(at.zp, at.h, 0, zp_own)
        self.send("u4", self.mine(at.zp, at.h, 0, 0), 3, 0, at.up, 0)
        self.pair(at.zm, at.h, 0, zm_own)
        self.send("d4", self.mine(at.zm, at.h, 0, 1), 4, 0, at.down, 1)
        self.pair(at.zz, at.h, 0, zz_own)
        z_other, z_own = self.compute(at.z, 0)
        self.factor(g_z)
        self.pair(at.z, at.hh, 0, z_other)
        self.pair(at.z, at.h, 0, z_own)

    def second(self):
        at = self.at
        zp_other, zp_own = self.compute(at.zp, 1)
        zm_other, zm_own = self.compute(at.zm, 1)
        self.pair(at.zp, at.hh, 1, zp_other)
        self.pair(at.zm, at.hh, 1, zm_other)
        self.cross(0)
        self.side(0)
        self.send("u5", self.mine(at.zp, at.hh, 1), 1, 1, at.up)
        self.send("d5", self.mine(at.zm, at.hh, 1), 2, 1, at.down)
        zz_other, zz_own = self.compute(at.zz, 1)
        self.pair(at.zp, at.h, 1, zp_own)
        self.pair(at.zm, at.h, 1, zm_own)
        self.pair(at.zz, at.hh, 1, zz_other)
        self.send("y1", self.mine(at.zz, at.hh, 1), 0, 1, at.across)
        self.join(0)
        self.send("u4", self.mine(at.zp, at.h, 1, 0), 3, 1, at.up, 0)
        self.send("d4", self.mine(at.zm, at.h, 1, 1), 4, 1, at.down, 1)
        self.pair(at.zz, at.h, 1, zz_own)
        z_other, z_own = self.compute(at.z, 1)
        self.pair(at.z, at.hh, 1, z_other)
        self.pair(at.z, at.h, 1, z_own)

    def cross(self, p):
        at = self.at
        self.arrived("y1", p)
        self.add(self.mine(at.zz, at.h, p), self.got.at[p, 0])
        self.send("c_down", self.mine(at.zz, at.h, p, 0), 5, p, at.down, 0)
        self.send("c_up", self.mine(at.zz, at.h, p, 1), 5, p, at.up, 1)

    def side(self, p):
        at = self.at
        self.arrived("u5", p)
        self.arrived("d5", p)
        self.add(self.mine(at.z, at.hh, p), self.got.at[p, 1], self.got.at[p, 2])
        self.send("y6", self.mine(at.z, at.hh, p), 6, p, at.across)

    def join(self, p):
        at = self.at
        self.arrived("c_down", p)
        self.add(self.mine(at.zm, at.h, p, 0), self.got.at[p, 5, pl.ds(0, 32)])
        self.send("d4", self.mine(at.zm, at.h, p, 0), 4, p, at.down, 0)
        self.arrived("c_up", p)
        self.add(self.mine(at.zp, at.h, p, 1), self.got.at[p, 5, pl.ds(32, 32)])
        self.send("u4", self.mine(at.zp, at.h, p, 1), 3, p, at.up, 1)

    def total(self, p, out):
        at = self.at
        for name in ("y6", "u4", "d4"):
            self.arrived(name, p)
        own = self.mine(at.z, at.h, p)

        def tile(n, carry):
            cols = pl.ds(aligned(n * 256, 256), 256)
            wide = pl.ds(aligned(p * HALF + n * 256, 256), 256)
            total = own[:, cols].astype(F32) + self.got[p, 6, :, cols].astype(F32)
            total = total + self.got[p, 3, :, cols].astype(F32) + self.got[p, 4, :, cols].astype(F32)
            out[:, wide] = total.astype(BF16)
            return carry

        lax.fori_loop(0, HALF // 256, tile, 0)


def kernel(
    inflow, fresh, wxz, wproj, wout_hbm, conv_w, conv_b, step_b, decay, skip, gain, out,
    act, raw, wout, weight, acc, proj, coded, sums, mixed, states, entering, window, gated, squares,
    part, from_sib, got, stats, scale, received, send_sem, recv_sem, local_sem,
):
    at = Place()
    pair = at.z // 2
    here = pl.ds(aligned(at.me * ROWS, ROWS), ROWS)
    loads = []
    for index, (src, dst) in enumerate(
        [
            (inflow, act.at[here]),
            (wxz.at[pl.ds(0, HALF)], raw.at[pl.ds(0, HALF)]),
            (wxz.at[pl.ds(HALF, HALF)], raw.at[pl.ds(HALF, HALF)]),
            (wproj.at[:, pl.ds(aligned(pair * 128, 128), 128)], weight.at[:, pl.ds(512, 128)]),
            (wproj.at[:, pl.ds(aligned(256 + pair * 128, 128), 128)], weight.at[:, pl.ds(640, 128)]),
            (wproj.at[:, pl.ds(512, 128)], weight.at[:, pl.ds(768, 128)]),
            (wout_hbm, wout),
        ]
    ):
        load = pltpu.make_async_copy(src, dst, local_sem.at[index])
        load.start()
        loads.append(load)
    at.meet()
    copies = Copies(send_sem, recv_sem)
    mixer = Mixer(
        at, (conv_w, conv_b, step_b, decay, skip, gain),
        proj, coded, sums, mixed, states, entering, window, gated, squares,
    )
    scatter_refs = (wout, part, from_sib, got, stats, scale)

    gather = Gather(at, copies, inflow, act, weight, acc, proj)
    gather.own(0)
    gather.own(1)

    def separate(p):
        loads[1 + p].wait()

        def tile(n, carry):
            at = pl.ds(aligned(p * HALF + n * 128, 128), 128)
            weight[at, pl.ds(0, CHAN)] = raw[at, 0, :]
            weight[at, pl.ds(CHAN, CHAN)] = raw[at, 1, :]
            return carry

        lax.fori_loop(0, HALF // 128, tile, 0)

    separate(0)
    gather.near(0)
    for index in (0, 3, 4, 5):
        loads[index].wait()

    @pl.when(at.sec == 0)
    def _():
        load = pltpu.make_async_copy(fresh, received, local_sem.at[0])
        load.start()
        load.wait()

    gather.rest(mixer, separate)
    loads[6].wait()
    copies.finish()

    scatter = Scatter(at, copies, mixer, *scatter_refs)
    hops = [copies.make(out.at[0, :, columns(p)], received.at[:, columns(p)], at.after) for p in (0, 1)]

    def relay(p):
        scatter.total(p, out.at[0])
        pl.when(at.sec < LAST)(hops[p].start)

    def relayed(p):
        pl.when(at.sec > 0)(hops[p].wait_recv)
        keep = pltpu.make_async_copy(
            received.at[:, columns(p)], act.at[here, columns(p)], local_sem.at[p]
        )
        keep.start()
        gather.own(p)
        return keep

    scatter.first()
    scatter.second()
    relay(0)
    scatter.cross(1)
    scatter.side(1)
    scatter.join(1)
    gather = Gather(at, copies, received, act, weight, acc, proj)
    keeps = [relayed(0)]
    relay(1)
    gather.near(0)
    keeps.append(relayed(1))
    for keep in keeps:
        keep.wait()
    gather.rest(mixer)
    for p in (0, 1):
        pl.when(at.sec < LAST)(hops[p].wait_send)
    copies.finish()

    scatter = Scatter(at, copies, mixer, *scatter_refs)
    scatter.first()
    scatter.second()
    scatter.cross(1)
    scatter.side(1)
    scatter.total(0, out.at[1])
    scatter.join(1)
    scatter.total(1, out.at[1])
    copies.finish()


def on_device(
    inflow,
    fresh,
    proj_weight,
    xz_weight,
    conv_weight,
    conv_bias,
    step_bias,
    decay_log,
    skip_weight,
    norm_gain,
    out_weight,
):
    anywhere = pl.BlockSpec(memory_space=pl.ANY)
    vmem = pl.BlockSpec(memory_space=pltpu.VMEM)
    out = pl.pallas_call(
        kernel,
        out_shape=jax.ShapeDtypeStruct((2, ROWS, WIDTH), BF16),
        in_specs=[anywhere] * 5 + [vmem] * 6,
        out_specs=vmem,
        scratch_shapes=[
            pltpu.VMEM((TOKENS, WIDTH), BF16),
            pltpu.VMEM((WIDTH, 2, CHAN), BF16),
            pltpu.VMEM((CHAN, WIDTH), BF16),
            pltpu.VMEM((WIDTH, COLS), BF16),
            pltpu.VMEM((TOKENS, COLS), F32),
            pltpu.VMEM((TOKENS + PAD, COLS), BF16),
            pltpu.VMEM((TOKENS, 128), BF16),
            pltpu.VMEM((TOKENS, CHAN), F32),
            pltpu.VMEM((TOKENS, CHAN), F32),
            pltpu.VMEM((TOKENS, CHAN), F32),
            pltpu.VMEM((TOKENS, CHAN), BF16),
            pltpu.VMEM((BLOCK + PAD, 512), F32),
            pltpu.VMEM((TOKENS, CHAN), BF16),
            pltpu.VMEM((8, TOKENS), F32),
            pltpu.VMEM((TOKENS, WIDTH), BF16),
            pltpu.VMEM((TOKENS // 2, WIDTH), BF16),
            pltpu.VMEM((2, LAST, ROWS, HALF), BF16),
            pltpu.VMEM((3, 8, TOKENS), F32),
            pltpu.VMEM((TOKENS, 128), F32),
            pltpu.VMEM((ROWS, WIDTH), BF16),
            pltpu.SemaphoreType.DMA((COPIES,)),
            pltpu.SemaphoreType.DMA((COPIES,)),
            pltpu.SemaphoreType.DMA((7,)),
        ],
        compiler_params=pltpu.CompilerParams(
            collective_id=0, has_side_effects=True, vmem_limit_bytes=60 * MIB
        ),
        name="relay_window",
    )(
        inflow[0], fresh[0], xz_weight[0], proj_weight[0], out_weight[0],
        conv_weight[0], conv_bias, step_bias, decay_log, skip_weight, norm_gain,
    )
    return out.astype(F32)[None]


def solution(mesh):
    placed = (
        P("section", "seq", None),
        P(None, "seq", None),
        P("section", None, None),
        P("section", None, None, "seq"),
        P("section", None, None),
        P("section", None),
        P("section", None),
        P("section", None),
        P("section", None),
        P("section", None),
        P("section", "seq", None),
    )
    return jax.shard_map(
        on_device,
        mesh=mesh,
        in_specs=placed,
        out_specs=P("section", None, "seq", None),
        check_vma=False,
    )
```

```python
import functools

import jax
import jax.numpy as jnp
from jax import lax
from jax.experimental import pallas as pl
from jax.experimental.pallas import tpu as pltpu
from jax.sharding import PartitionSpec as P

MESH = pl.DeviceIdType.MESH
F32 = jnp.float32
BF16 = jnp.bfloat16
HIGHEST = lax.Precision.HIGHEST
TOKENS = 1024
WIDTH = 4096
CHAN = 256
BLOCK = 128
BLOCKS = TOKENS // BLOCK
ROWS = 64
HALF = WIDTH // 2
COLS = 896
TILES = ((0, 256), (256, 256), (512, 256), (768, 128))
LAST = 7
PAD = 16
COPIES = 192
MIB = 2**20


def aligned(value, by):
    return pl.multiple_of(value, by)


def iota(shape, dim):
    return lax.broadcasted_iota(jnp.int32, shape, dim)


def columns(p):
    return pl.ds(p * HALF, HALF)


def parts_of(value, count):
    parts = []
    for _ in range(count):
        part = value.astype(BF16)
        parts.append(part)
        value = value - part.astype(F32)
    return parts


class Place:
    def __init__(self):
        self.sec = lax.axis_index("section")
        self.me = lax.axis_index("seq")
        self.z, self.h, self.c = self.me // 4, (self.me // 2) % 2, self.me % 2
        self.zp, self.zm, self.zz = (self.z + 1) % 4, (self.z + 3) % 4, (self.z + 2) % 4
        self.hh = 1 - self.h
        self.up = self.device(self.zp, self.h, self.c)
        self.down = self.device(self.zm, self.h, self.c)
        self.across = self.device(self.z, self.hh, self.c)
        self.sib = self.device(self.z, self.h, 1 - self.c)
        self.diag = self.device(self.z, self.hh, 1 - self.c)
        self.after = ((self.sec + 1) % 8, self.me)
        self.ahead = ((self.sec + 7) % 8, self.me)

    def device(self, z, h, c):
        return (self.sec, z * 4 + h * 2 + c)

    def meet(self):
        targets = [self.up, self.down, self.across, self.sib, self.diag, self.after, self.ahead]
        barrier = pltpu.get_barrier_semaphore()
        for target in targets:
            pl.semaphore_signal(barrier, inc=1, device_id=target, device_id_type=MESH)
        pl.semaphore_wait(barrier, len(targets))


class Copies:
    def __init__(self, send_sem, recv_sem):
        self.send_sem, self.recv_sem = send_sem, recv_sem
        self.count = 0
        self.open = []

    def make(self, src, dst, target):
        index = self.count
        self.count += 1
        return pltpu.make_async_remote_copy(
            src_ref=src,
            dst_ref=dst,
            send_sem=self.send_sem.at[index],
            recv_sem=self.recv_sem.at[index],
            device_id=target,
            device_id_type=MESH,
        )

    def new(self, src, dst, target):
        copy = self.make(src, dst, target)
        copy.start()
        self.open.append(copy)
        return copy

    def finish(self):
        for copy in self.open:
            copy.wait_send()
        self.open = []


class Gather:
    def __init__(self, at, copies, source, act, weight, acc, proj):
        self.at, self.copies, self.source = at, copies, source
        self.act, self.weight, self.acc, self.proj = act, weight, acc, proj
        self.got = {}

    def rows(self, z, h, p, half=None):
        start = (z * 2 + h) * 128 + self.at.c * ROWS
        if half is None:
            return self.act.at[pl.ds(aligned(start, ROWS), ROWS), columns(p)]
        return self.act.at[pl.ds(aligned(start + half * 32, 32), 32), columns(p)]

    def forward(self, z, h, p, target, half=None):
        return self.copies.new(self.rows(z, h, p, half), self.rows(z, h, p, half), target)

    def share(self, name, z, h, p, half=None):
        self.got.setdefault((name, p), []).append(self.forward(z, h, p, self.at.sib, half))

    def own(self, p):
        at = self.at
        src = self.source.at[:, columns(p)]
        dst = self.rows(at.z, at.h, p)
        for name, target in (("up", at.up), ("down", at.down), ("across", at.across), ("own", at.sib)):
            self.got[name, p] = [self.copies.new(src, dst, target)]

    def arrived(self, name, p):
        for copy in self.got[name, p]:
            copy.wait_recv()

    def near(self, p):
        at = self.at
        self.arrived("up", p)
        self.got["cu", p] = [self.forward(at.zm, at.h, p, at.up, 0)]
        self.arrived("down", p)
        self.got["cd", p] = [self.forward(at.zp, at.h, p, at.down, 1)]
        self.share("s_zm", at.zm, at.h, p)
        self.share("s_zp", at.zp, at.h, p)
        self.arrived("across", p)
        self.got["pu", p] = [self.forward(at.z, at.hh, p, at.up)]
        self.got["pd", p] = [self.forward(at.z, at.hh, p, at.down)]
        self.share("s_p", at.z, at.hh, p)

    def far(self, p):
        at = self.at
        for name, half in (("cu", 0), ("cd", 1)):
            self.arrived(name, p)
            self.got["cy%d" % half, p] = [self.forward(at.zz, at.h, p, at.across, half)]
            self.share("s_c", at.zz, at.h, p, half)

    def beside(self, p):
        at = self.at
        self.arrived("pu", p)
        self.share("s_pm", at.zm, at.hh, p)
        self.arrived("pd", p)
        self.share("s_pp", at.zp, at.hh, p)

    def last(self, p):
        at = self.at
        for half in (0, 1):
            self.arrived("cy%d" % half, p)
            self.share("s_cy", at.zz, at.hh, p, half)

    def project(self, name, z, h, p):
        self.arrived(name, p)
        start = (z * 2 + h) * 128
        at = pl.ds(aligned(start, 128), 128)
        padded = pl.ds(aligned(start + PAD, PAD), 128)
        for first, size in TILES:
            cols = pl.ds(first, size)
            part = jnp.dot(
                self.act[at, columns(p)], self.weight[columns(p), cols], preferred_element_type=F32
            )
            if p == 0:
                self.acc[at, cols] = part
            else:
                self.proj[padded, cols] = (self.acc[at, cols] + part).astype(BF16)

    def project_near(self, p):
        at = self.at
        self.project("own", at.z, at.h, p)
        self.project("s_zm", at.zm, at.h, p)
        self.project("s_zp", at.zp, at.h, p)
        self.project("s_p", at.z, at.hh, p)

    def project_beside(self, p):
        at = self.at
        self.project("s_pm", at.zm, at.hh, p)
        self.project("s_pp", at.zp, at.hh, p)

    def rest(self, mixer, separate=None):
        at = self.at
        self.project_near(0)
        self.near(1)
        self.far(0)
        if separate is not None:
            separate(1)
        self.project_near(1)
        self.beside(0)
        self.project("s_c", at.zz, at.h, 0)
        self.far(1)
        mixer.local(0)
        self.project_beside(0)
        self.last(0)
        self.project("s_c", at.zz, at.h, 1)
        self.beside(1)
        self.project("s_cy", at.zz, at.hh, 0)
        self.project_beside(1)
        mixer.local(1)
        self.last(1)
        mixer.local(2)
        self.project("s_cy", at.zz, at.hh, 1)
        mixer.local(3)
        mixer.chain()


class Mixer:
    def __init__(self, at, params, proj, coded, sums, mixed, states, entering, window, gated, squares):
        self.proj, self.coded, self.sums, self.mixed = proj, coded, sums, mixed
        self.states, self.entering, self.window = states, entering, window
        self.gated, self.squares = gated, squares
        conv_w, conv_b, step_b, decay, skip, gain = params
        group = at.me // 4
        x_at = aligned(at.me * CHAN, CHAN)
        b_at = aligned(4096 + (group // 2) * 128, 128)
        c_at = aligned(4352 + (group // 2) * 128, 128)

        def own(ref):
            return jnp.concatenate(
                [ref[:, pl.ds(x_at, CHAN)], ref[:, pl.ds(b_at, 128)], ref[:, pl.ds(c_at, 128)]], axis=1
            )

        spread = (iota((128, CHAN), 0) == at.me * 8 + iota((128, CHAN), 1) // 32).astype(F32)

        def per_channel(ref):
            wide = jnp.broadcast_to(ref[...], (8, 128))
            return jnp.dot(wide, spread, precision=HIGHEST, preferred_element_type=F32)[0:1]

        self.taps, self.offset = own(conv_w), own(conv_b)
        self.bias = per_channel(step_b)
        self.rate = -jnp.exp(per_channel(decay))
        self.direct = per_channel(skip)
        self.gains = gain[:, pl.ds(x_at, CHAN)]
        self.spread = spread.astype(BF16)
        self.half = group % 2
        one, two = at.hh, at.h
        self.order = [
            one * (2 * at.z + 1) + two * (2 * at.z),
            one * (2 * at.zp) + two * (2 * at.z + 1),
            one * (2 * at.z) + two * (2 * at.zp),
            one * (2 * at.zm + 1) + two * (2 * at.zp + 1),
            one * (2 * at.zp + 1) + two * (2 * at.zm),
            one * (2 * at.zz) + two * (2 * at.zm + 1),
            one * (2 * at.zm) + two * (2 * at.zz),
            2 * at.zz + 1,
        ]
        proj[0:PAD, :] = jnp.zeros((PAD, COLS), BF16)

    def local(self, pair):
        first, second = self.order[2 * pair], self.order[2 * pair + 1]
        taps, window = self.taps, self.window
        lower = iota((BLOCK, BLOCK), 0) >= iota((BLOCK, BLOCK), 1)
        lower_ones = lower.astype(F32).astype(BF16)
        own_half = iota((BLOCK, 128), 1) // 64 == self.half
        head_of = iota((BLOCK, CHAN), 1) // 32

        def block(index, carry):
            start = ((1 - index) * first + index * second) * BLOCK
            at = pl.ds(aligned(start, BLOCK), BLOCK)
            rows = pl.ds(aligned(start + PAD, PAD), BLOCK)
            window[0:PAD, :] = self.proj[pl.ds(aligned(start, PAD), PAD), pl.ds(256, 512)].astype(F32)
            window[PAD : PAD + BLOCK, :] = self.proj[rows, pl.ds(256, 512)].astype(F32)
            conv = self.offset + taps[0:1] * window[PAD - 3 : PAD - 3 + BLOCK, :]
            for k in range(1, 4):
                conv = conv + taps[k : k + 1] * window[PAD - 3 + k : PAD - 3 + k + BLOCK, :]
            conv = (conv / (1.0 + jnp.exp(-conv))).astype(BF16)
            x = conv[:, :CHAN]
            b = conv[:, CHAN : CHAN + 128]
            c = jnp.where(own_half, conv[:, CHAN + 128 :], jnp.zeros((), BF16))
            self.coded[at, :] = c
            step = jax.nn.softplus(
                jnp.dot(self.proj[rows, pl.ds(768, 128)], self.spread, preferred_element_type=F32)
                + self.bias
            )
            cumulus = jnp.zeros((BLOCK, CHAN), F32)
            for part in parts_of(self.rate * step, 3):
                cumulus = cumulus + jnp.dot(lower_ones, part, preferred_element_type=F32)
            self.sums[at, :] = cumulus
            cumulus_t = cumulus.T
            step_t = step.T
            scores = lax.dot_general(c, b, (((1,), (1,)), ((), ())), preferred_element_type=F32)
            mixing, values = [], []
            for head in range(8):
                lane = 32 * head
                gap = cumulus[:, lane : lane + 1] - cumulus_t[lane : lane + 1, :]
                gap = jnp.where(lower, gap, -1e30)
                mixing.append((scores * jnp.exp(gap) * step_t[lane : lane + 1, :]).astype(BF16))
                values.append(jnp.where(head_of == head, x, jnp.zeros((), BF16)))
            diagonal = jnp.dot(
                jnp.concatenate(mixing, axis=1),
                jnp.concatenate(values, axis=0),
                preferred_element_type=F32,
            )
            x32 = x.astype(F32)
            self.mixed[at, :] = diagonal + self.direct * x32
            total = cumulus[BLOCK - 1 : BLOCK]
            weighted = (x32 * (jnp.exp(total - cumulus) * step)).astype(BF16)
            self.states[at, :] = lax.dot_general(
                b, weighted, (((0,), (0,)), ((), ())), preferred_element_type=F32
            )
            return carry

        lax.fori_loop(0, 2, block, 0)

    def chain(self):
        state = jnp.zeros((BLOCK, CHAN), F32)
        for index in range(BLOCKS):
            at = pl.ds(index * BLOCK, BLOCK)
            self.entering[at, :] = state.astype(BF16)
            if index < BLOCKS - 1:
                total = self.sums[(index + 1) * BLOCK - 1 : (index + 1) * BLOCK, :]
                state = jnp.exp(total) * state + self.states[at, :]

    def outputs(self, z):
        def block(index, carry):
            start = z * 256 + index * BLOCK
            at = pl.ds(aligned(start, BLOCK), BLOCK)
            mixed = self.mixed[at, :] + jnp.exp(self.sums[at, :]) * jnp.dot(
                self.coded[at, :], self.entering[at, :], preferred_element_type=F32
            )
            gate = self.proj[pl.ds(aligned(start + PAD, PAD), BLOCK), pl.ds(0, CHAN)].astype(F32)
            gated = mixed * (gate / (1.0 + jnp.exp(-gate)))
            total = jnp.zeros((8, BLOCK), F32)
            for part in parts_of(gated * gated, 2):
                total = total + lax.dot_general(
                    jnp.ones((8, CHAN), BF16), part, (((1,), (1,)), ((), ())), preferred_element_type=F32
                )
            self.squares[:, at] = total
            self.gated[at, :] = (gated * self.gains).astype(BF16)
            return carry

        lax.fori_loop(0, 2, block, 0, unroll=True)


class Scatter:
    def __init__(self, at, copies, mixer, wout, part, from_sib, got, stats, scale):
        self.at, self.copies, self.mixer, self.wout = at, copies, mixer, wout
        self.part, self.from_sib, self.got, self.stats, self.scale = part, from_sib, got, stats, scale
        self.sent = {}

    def gate(self, z):
        self.mixer.outputs(z)
        cols = pl.ds(aligned(z * 256, 256), 256)
        squares = self.mixer.squares.at[:, cols]
        self.shares = [
            self.copies.new(squares, self.stats.at[i, :, cols], target)
            for i, target in enumerate((self.at.sib, self.at.across, self.at.diag))
        ]
        return z, self.shares

    def factor(self, gate):
        z, shares = gate
        for share in shares:
            share.wait_recv()
        for i in (0, 1):
            at = pl.ds(aligned(z * 256 + i * 128, 128), 128)
            total = self.mixer.squares[:, at] + self.stats[0, :, at]
            total = total + self.stats[1, :, at] + self.stats[2, :, at]
            self.scale[at, :] = lax.dot_general(
                lax.rsqrt(total / 1024.0 + 1e-05),
                jnp.full((8, 128), 0.125, F32),
                (((0,), (0,)), ((), ())),
                precision=HIGHEST,
                preferred_element_type=F32,
            )

    def mine(self, z, h, p, half=None):
        start = (z * 2 + h) * 128 + self.at.c * ROWS
        if half is None:
            return self.part.at[pl.ds(aligned(start, ROWS), ROWS), columns(p)]
        return self.part.at[pl.ds(aligned(start + half * 32, 32), 32), columns(p)]

    def compute(self, z, p):
        at = pl.ds(aligned(z * 256, 256), 256)
        lhs = self.mixer.gated[at, :]

        def tile(n, carry):
            cols = pl.ds(aligned(p * HALF + n * 512, 512), 512)
            self.part[at, cols] = jnp.dot(
                lhs, self.wout[:, cols], preferred_element_type=F32
            ).astype(BF16)
            return carry

        lax.fori_loop(0, HALF // 512, tile, 0)
        copies = []
        for h in (self.at.hh, self.at.h):
            start = (z * 2 + h) * 128 + (1 - self.at.c) * ROWS
            src = self.part.at[pl.ds(aligned(start, ROWS), ROWS), columns(p)]
            dst = self.from_sib.at[pl.ds(aligned((z * 2 + h) * ROWS, ROWS), ROWS), columns(p)]
            copies.append(self.copies.new(src, dst, self.at.sib))
        return copies

    def pair(self, z, h, p, copy):
        copy.wait_recv()
        own = self.mine(z, h, p)
        other = self.from_sib.at[pl.ds(aligned((z * 2 + h) * ROWS, ROWS), ROWS), columns(p)]
        rows = pl.ds(aligned((z * 2 + h) * 128 + self.at.c * ROWS, ROWS), ROWS)
        scale = jnp.concatenate([self.scale[rows, :]] * 2, axis=1)

        def tile(n, carry):
            cols = pl.ds(aligned(n * 256, 256), 256)
            total = own[:, cols].astype(F32) + other[:, cols].astype(F32)
            own[:, cols] = (total * scale).astype(BF16)
            return carry

        lax.fori_loop(0, HALF // 256, tile, 0)

    @staticmethod
    def add(dst, *others):
        def tile(n, carry):
            cols = pl.ds(aligned(n * 256, 256), 256)
            total = dst[:, cols].astype(F32)
            for other in others:
                total = total + other[:, cols].astype(F32)
            dst[:, cols] = total.astype(BF16)
            return carry

        lax.fori_loop(0, HALF // 256, tile, 0)

    def send(self, name, src, slot, p, target, half=None):
        dst = self.got.at[p, slot]
        if half is not None:
            dst = self.got.at[p, slot, pl.ds(half * 32, 32)]
        self.sent.setdefault((name, p), []).append(self.copies.new(src, dst, target))

    def arrived(self, name, p):
        for copy in self.sent[name, p]:
            copy.wait_recv()

    def first(self):
        at = self.at
        g_zp = self.gate(at.zp)
        g_zm = self.gate(at.zm)
        zp_other, zp_own = self.compute(at.zp, 0)
        zm_other, zm_own = self.compute(at.zm, 0)
        g_zz = self.gate(at.zz)
        self.factor(g_zp)
        self.pair(at.zp, at.hh, 0, zp_other)
        self.send("u5", self.mine(at.zp, at.hh, 0), 1, 0, at.up)
        self.factor(g_zm)
        self.pair(at.zm, at.hh, 0, zm_other)
        self.send("d5", self.mine(at.zm, at.hh, 0), 2, 0, at.down)
        zz_other, zz_own = self.compute(at.zz, 0)
        g_z = self.gate(at.z)
        self.factor(g_zz)
        self.pair(at.zz, at.hh, 0, zz_other)
        self.send("y1", self.mine(at.zz, at.hh, 0), 0, 0, at.across)
        self.pair(at.zp, at.h, 0, zp_own)
        self.send("u4", self.mine(at.zp, at.h, 0, 0), 3, 0, at.up, 0)
        self.pair(at.zm, at.h, 0, zm_own)
        self.send("d4", self.mine(at.zm, at.h, 0, 1), 4, 0, at.down, 1)
        self.pair(at.zz, at.h, 0, zz_own)
        z_other, z_own = self.compute(at.z, 0)
        self.factor(g_z)
        self.pair(at.z, at.hh, 0, z_other)
        self.pair(at.z, at.h, 0, z_own)

    def second(self):
        at = self.at
        zp_other, zp_own = self.compute(at.zp, 1)
        zm_other, zm_own = self.compute(at.zm, 1)
        self.pair(at.zp, at.hh, 1, zp_other)
        self.pair(at.zm, at.hh, 1, zm_other)
        self.cross(0)
        self.side(0)
        self.send("u5", self.mine(at.zp, at.hh, 1), 1, 1, at.up)
        self.send("d5", self.mine(at.zm, at.hh, 1), 2, 1, at.down)
        zz_other, zz_own = self.compute(at.zz, 1)
        self.pair(at.zp, at.h, 1, zp_own)
        self.pair(at.zm, at.h, 1, zm_own)
        self.pair(at.zz, at.hh, 1, zz_other)
        self.send("y1", self.mine(at.zz, at.hh, 1), 0, 1, at.across)
        self.join(0)
        self.send("u4", self.mine(at.zp, at.h, 1, 0), 3, 1, at.up, 0)
        self.send("d4", self.mine(at.zm, at.h, 1, 1), 4, 1, at.down, 1)
        self.pair(at.zz, at.h, 1, zz_own)
        z_other, z_own = self.compute(at.z, 1)
        self.pair(at.z, at.hh, 1, z_other)
        self.pair(at.z, at.h, 1, z_own)

    def cross(self, p):
        at = self.at
        self.arrived("y1", p)
        self.add(self.mine(at.zz, at.h, p), self.got.at[p, 0])
        self.send("c_down", self.mine(at.zz, at.h, p, 0), 5, p, at.down, 0)
        self.send("c_up", self.mine(at.zz, at.h, p, 1), 5, p, at.up, 1)

    def side(self, p):
        at = self.at
        self.arrived("u5", p)
        self.arrived("d5", p)
        self.add(self.mine(at.z, at.hh, p), self.got.at[p, 1], self.got.at[p, 2])
        self.send("y6", self.mine(at.z, at.hh, p), 6, p, at.across)

    def join(self, p):
        at = self.at
        self.arrived("c_down", p)
        self.add(self.mine(at.zm, at.h, p, 0), self.got.at[p, 5, pl.ds(0, 32)])
        self.send("d4", self.mine(at.zm, at.h, p, 0), 4, p, at.down, 0)
        self.arrived("c_up", p)
        self.add(self.mine(at.zp, at.h, p, 1), self.got.at[p, 5, pl.ds(32, 32)])
        self.send("u4", self.mine(at.zp, at.h, p, 1), 3, p, at.up, 1)

    def total(self, p, out):
        at = self.at
        for name in ("y6", "u4", "d4"):
            self.arrived(name, p)
        own = self.mine(at.z, at.h, p)

        def tile(n, carry):
            cols = pl.ds(aligned(n * 256, 256), 256)
            wide = pl.ds(aligned(p * HALF + n * 256, 256), 256)
            total = own[:, cols].astype(F32) + self.got[p, 6, :, cols].astype(F32)
            total = total + self.got[p, 3, :, cols].astype(F32) + self.got[p, 4, :, cols].astype(F32)
            out[:, wide] = total.astype(BF16)
            return carry

        lax.fori_loop(0, HALF // 256, tile, 0)


def kernel(
    inflow, fresh, wxz, wproj, wout_hbm, conv_w, conv_b, step_b, decay, skip, gain, out,
    act, raw, wout, weight, acc, proj, coded, sums, mixed, states, entering, window, gated, squares,
    part, from_sib, got, stats, scale, received, send_sem, recv_sem, local_sem,
):
    at = Place()
    pair = at.z // 2
    here = pl.ds(aligned(at.me * ROWS, ROWS), ROWS)
    loads = []
    for index, (src, dst) in enumerate(
        [
            (inflow, act.at[here]),
            (wxz.at[pl.ds(0, HALF)], raw.at[pl.ds(0, HALF)]),
            (wxz.at[pl.ds(HALF, HALF)], raw.at[pl.ds(HALF, HALF)]),
            (wproj.at[:, pl.ds(aligned(pair * 128, 128), 128)], weight.at[:, pl.ds(512, 128)]),
            (wproj.at[:, pl.ds(aligned(256 + pair * 128, 128), 128)], weight.at[:, pl.ds(640, 128)]),
            (wproj.at[:, pl.ds(512, 128)], weight.at[:, pl.ds(768, 128)]),
            (wout_hbm, wout),
        ]
    ):
        load = pltpu.make_async_copy(src, dst, local_sem.at[index])
        load.start()
        loads.append(load)
    at.meet()
    copies = Copies(send_sem, recv_sem)
    mixer = Mixer(
        at, (conv_w, conv_b, step_b, decay, skip, gain),
        proj, coded, sums, mixed, states, entering, window, gated, squares,
    )
    scatter_refs = (wout, part, from_sib, got, stats, scale)

    gather = Gather(at, copies, inflow, act, weight, acc, proj)
    gather.own(0)
    gather.own(1)

    def separate(p):
        loads[1 + p].wait()

        def tile(n, carry):
            at = pl.ds(aligned(p * HALF + n * 128, 128), 128)
            weight[at, pl.ds(0, CHAN)] = raw[at, 0, :]
            weight[at, pl.ds(CHAN, CHAN)] = raw[at, 1, :]
            return carry

        lax.fori_loop(0, HALF // 128, tile, 0)

    separate(0)
    gather.near(0)
    for index in (0, 3, 4, 5):
        loads[index].wait()

    @pl.when(at.sec == 0)
    def _():
        load = pltpu.make_async_copy(fresh, received, local_sem.at[0])
        load.start()
        load.wait()

    gather.rest(mixer, separate)
    loads[6].wait()
    copies.finish()

    scatter = Scatter(at, copies, mixer, *scatter_refs)
    hops = [copies.make(out.at[0, :, columns(p)], received.at[:, columns(p)], at.after) for p in (0, 1)]

    def relay(p):
        scatter.total(p, out.at[0])
        pl.when(at.sec < LAST)(hops[p].start)

    def relayed(p):
        pl.when(at.sec > 0)(hops[p].wait_recv)
        keep = pltpu.make_async_copy(
            received.at[:, columns(p)], act.at[here, columns(p)], local_sem.at[p]
        )
        keep.start()
        gather.own(p)
        return keep

    scatter.first()
    scatter.second()
    relay(0)
    scatter.cross(1)
    scatter.side(1)
    scatter.join(1)
    gather = Gather(at, copies, received, act, weight, acc, proj)
    keeps = [relayed(0)]
    relay(1)
    gather.near(0)
    keeps.append(relayed(1))
    for keep in keeps:
        keep.wait()
    gather.rest(mixer)
    for p in (0, 1):
        pl.when(at.sec < LAST)(hops[p].wait_send)
    copies.finish()

    scatter = Scatter(at, copies, mixer, *scatter_refs)
    scatter.first()
    scatter.second()
    scatter.cross(1)
    scatter.side(1)
    scatter.total(0, out.at[1])
    scatter.join(1)
    scatter.total(1, out.at[1])
    copies.finish()


def on_device(
    inflow,
    fresh,
    proj_weight,
    xz_weight,
    conv_weight,
    conv_bias,
    step_bias,
    decay_log,
    skip_weight,
    norm_gain,
    out_weight,
):
    anywhere = pl.BlockSpec(memory_space=pl.ANY)
    vmem = pl.BlockSpec(memory_space=pltpu.VMEM)
    out = pl.pallas_call(
        kernel,
        out_shape=jax.ShapeDtypeStruct((2, ROWS, WIDTH), BF16),
        in_specs=[anywhere] * 5 + [vmem] * 6,
        out_specs=vmem,
        scratch_shapes=[
            pltpu.VMEM((TOKENS, WIDTH), BF16),
            pltpu.VMEM((WIDTH, 2, CHAN), BF16),
            pltpu.VMEM((CHAN, WIDTH), BF16),
            pltpu.VMEM((WIDTH, COLS), BF16),
            pltpu.VMEM((TOKENS, COLS), F32),
            pltpu.VMEM((TOKENS + PAD, COLS), BF16),
            pltpu.VMEM((TOKENS, 128), BF16),
            pltpu.VMEM((TOKENS, CHAN), F32),
            pltpu.VMEM((TOKENS, CHAN), F32),
            pltpu.VMEM((TOKENS, CHAN), F32),
            pltpu.VMEM((TOKENS, CHAN), BF16),
            pltpu.VMEM((BLOCK + PAD, 512), F32),
            pltpu.VMEM((TOKENS, CHAN), BF16),
            pltpu.VMEM((8, TOKENS), F32),
            pltpu.VMEM((TOKENS, WIDTH), BF16),
            pltpu.VMEM((TOKENS // 2, WIDTH), BF16),
            pltpu.VMEM((2, LAST, ROWS, HALF), BF16),
            pltpu.VMEM((3, 8, TOKENS), F32),
            pltpu.VMEM((TOKENS, 128), F32),
            pltpu.VMEM((ROWS, WIDTH), BF16),
            pltpu.SemaphoreType.DMA((COPIES,)),
            pltpu.SemaphoreType.DMA((COPIES,)),
            pltpu.SemaphoreType.DMA((7,)),
        ],
        compiler_params=pltpu.CompilerParams(
            collective_id=0, has_side_effects=True, vmem_limit_bytes=60 * MIB
        ),
        name="relay_window",
    )(
        inflow[0], fresh[0], xz_weight[0], proj_weight[0], out_weight[0],
        conv_weight[0], conv_bias, step_bias, decay_log, skip_weight, norm_gain,
    )
    return out.astype(F32)[None]


def solution(mesh):
    placed = (
        P("section", "seq", None),
        P(None, "seq", None),
        P("section", None, None),
        P("section", None, None, "seq"),
        P("section", None, None),
        P("section", None),
        P("section", None),
        P("section", None),
        P("section", None),
        P("section", None),
        P("section", "seq", None),
    )
    return jax.shard_map(
        on_device,
        mesh=mesh,
        in_specs=placed,
        out_specs=P("section", None, "seq", None),
        check_vma=False,
    )
```
